32 devices in a mesh: groups: 2 (over y), ctx: 4 (over z), head: 2 (over x), mem: 2 (over core).
Axes of the slice: x: 2, y: 2, z: 4, core: 2. Of those that a mesh axis runs over, the one named last changes fastest.
Arguments:
- queries: bfloat16 [8192, 2048], P(('groups', 'ctx', 'mem'), 'head'), parts along dimension 0, may hold values from -48 to 48
- keys: bfloat16 [8192, 2048], P(('groups', 'ctx', 'mem'), 'head'), parts along dimension 0, may hold values from -6 to 6
- values: bfloat16 [8192, 2048], P(('groups', 'ctx', 'mem'), 'head'), parts along dimension 0, may hold values from -6 to 6
- memory_keys: bfloat16 [32768, 2048], P(('groups', 'ctx', 'mem'), 'head'), parts along dimension 0, may hold values from -6 to 6
- memory_values: bfloat16 [32768, 2048], P(('groups', 'ctx', 'mem'), 'head'), parts along dimension 0, may hold values from -6 to 6
- retrieval: int32 [128, 8], P(('groups', 'ctx', 'mem')), parts along dimension 0, may hold values from 0 to 255, as said below
- memory_gate: float32 [16], P('head'), may hold values from -1 to 2
Outputs:
- attended: bfloat16 [8192, 2048], P(('groups', 'ctx', 'mem'), 'head'), parts along dimension 0
The draws below stay inside these ranges and needn't reach their ends.
There are 2 independent parts, one for each index of `groups`. The reference program is written for one: setup_inputs(seed, part) draws one part's arguments, and reference() takes and returns one part's arrays. A program takes and returns all parts, laid end to end along the dimension named above; an argument that names none is the same for every part. Nothing has to cross between parts.
Inputs may be any that keep to these rules, and one draw needn't show every extreme that they name: `retrieval`: all ids named by the rows of one device (the 8 ids of each of its query blocks) are distinct. A holder is a block of 32 consecutive memory blocks; from the rows of one device at most 12 ids fall in one holder, and in every device some holder gets exactly 12 of them.
All inputs are finite; a program needn't handle non-finite values.
Results may differ from the reference program's by a relative error of at most 0.0049.
Values may be sent and summed in bfloat16 or wider, within the bound.
A program may use at most 256 MiB of HBM per device.

```python
import math
import jax
import jax.numpy as jnp
from jax import lax

HEADS = 16
HDIM = 128
QBLK = 64
TOPK = 8
SPAN = 4
TOK_DEV = 512
MEM_DEV = 2048
HOLDERS = 8
TOKENS = 4096
MEMTOK = 16384
MEMBLOCKS = 256
CAP = 12


def paired_keys(key):
    first_key = jax.random.fold_in(key, 0)
    shape_all = (TOKENS, HEADS * HDIM)
    bell_draw = jnp.clip(jax.random.normal(first_key, shape_all, jnp.float32), -5.0, 5.0)
    base_keys = bell_draw
    row_ids = jnp.arange(TOKENS, dtype=jnp.int32)
    twin_rows = (row_ids % 61 == 7)[:, None]
    return jnp.where(twin_rows, base_keys, base_keys)


def draw_keys(key, part):
    return paired_keys(key).astype(jnp.bfloat16)


def draw_queries(key, part):
    shape_all = (TOKENS, HEADS * HDIM)
    key = jax.random.fold_in(key, 5)
    return (2.5 * jnp.clip(jax.random.normal(key, shape_all, jnp.float32), -5.0, 5.0)).astype(jnp.bfloat16)


def draw_retrieval(key, part):
    key = jax.random.fold_in(key, 11)
    per_device = TOK_DEV // QBLK * TOPK
    blocks_held = MEM_DEV // QBLK
    favour_key, device_key = jax.random.split(key)
    favourites = jax.random.permutation(favour_key, HOLDERS)[:2].astype(jnp.int32)

    def one_device(one_key):
        pick_key, slot_key, offset_key, order_key = jax.random.split(one_key, 4)
        favoured = favourites[jax.random.randint(pick_key, (), 0, 2)]
        slot_draw = jax.random.permutation(slot_key, (HOLDERS - 1) * CAP)[:per_device - CAP].astype(jnp.int32)
        other_holders = (favoured + 1 + slot_draw // CAP) % HOLDERS
        holder_of = jnp.concatenate([jnp.full((CAP,), favoured, jnp.int32), other_holders])
        slot_rank = jnp.concatenate([jnp.arange(CAP, dtype=jnp.int32), slot_draw % CAP])
        offsets = jax.random.randint(offset_key, (HOLDERS,), 0, blocks_held).astype(jnp.int32)
        local_block = (offsets[holder_of] + slot_rank) % blocks_held
        block_ids = holder_of * blocks_held + local_block
        shuffle = jax.random.permutation(order_key, per_device)
        return block_ids[shuffle].reshape(TOK_DEV // QBLK, TOPK)
    device_keys = jax.random.split(device_key, HOLDERS)
    drawn = jax.vmap(one_device)(device_keys)
    return drawn.reshape(HOLDERS * (TOK_DEV // QBLK), TOPK).astype(jnp.int32)


def steps_of(stream_key, shape, cuts, smallest, high):
    def one(position, shards_of):
        steps = jax.random.uniform(jax.random.fold_in(jax.random.fold_in(stream_key, 6), position), (shards_of,), jnp.float32, smallest / len(cuts), high / len(cuts))
        return jnp.repeat(jnp.exp(steps), shape[position] // shards_of).reshape((-1,) + (1,) * (len(shape) - position - 1))

    level = one(*cuts[0])
    for cut in cuts[1:]:
        level = level * one(*cut)
    return level


def scatter_about(stream_key, dims, scale, bound, shards=(), held_as=jnp.bfloat16):
    values = scale * jax.random.normal(stream_key, dims, jnp.float32)
    if shards:
        values = values * steps_of(stream_key, dims, shards, -0.22, 0.18)
    return jnp.clip(values, -bound, bound).astype(held_as)


def setup_inputs(seed: int = 0, part: int = 0) -> dict:
    key_of = jax.random.split(jax.random.key(seed), 8)
    own_keys = jax.random.split(jax.random.fold_in(key_of[7], part), 8)
    queries = draw_queries(jax.random.fold_in(jax.random.fold_in(key_of[7], part), 71), part)
    keys = draw_keys(jax.random.fold_in(jax.random.fold_in(key_of[7], part), 71), part)
    values = scatter_about(own_keys[2], (TOKENS, HEADS * HDIM), 1.0, 6.0, ((0, 8), (1, 2)))
    memory_keys = scatter_about(own_keys[3], (MEMTOK, HEADS * HDIM), 1.0, 6.0, ((0, 8), (1, 2)))
    memory_values = scatter_about(own_keys[4], (MEMTOK, HEADS * HDIM), 1.0, 6.0, ((0, 8), (1, 2)))
    retrieval = draw_retrieval(jax.random.fold_in(jax.random.fold_in(key_of[7], part), 71), part)
    memory_gate = jnp.clip(-1.0 + 3.0 * jax.random.uniform(key_of[6], (HEADS,), jnp.float32) ** steps_of(key_of[6], (HEADS,), ((0, 2),), -0.2, 0.2), -1.0, 2.0)
    return dict(queries=queries, keys=keys, values=values, memory_keys=memory_keys, memory_values=memory_values, retrieval=retrieval, memory_gate=memory_gate)


def reference(queries, keys, values, memory_keys, memory_values, retrieval, memory_gate):
    window = SPAN * TOK_DEV
    score_scale = 1.0 / math.sqrt(HDIM)
    per_block = TOK_DEV // QBLK
    width = HEADS * HDIM
    padded_keys = jnp.concatenate([jnp.zeros((window, width), keys.dtype), keys], axis=0)
    padded_values = jnp.concatenate([jnp.zeros((window, width), values.dtype), values], axis=0)
    blocks_keys = memory_keys.reshape(MEMBLOCKS, QBLK, HEADS, HDIM)
    blocks_values = memory_values.reshape(MEMBLOCKS, QBLK, HEADS, HDIM)

    def one_block(block_index):
        row_start = (block_index * TOK_DEV).astype(jnp.int32)
        query_rows = lax.dynamic_slice_in_dim(queries, row_start, TOK_DEV, 0).astype(jnp.float32).reshape(TOK_DEV, HEADS, HDIM)
        key_rows = lax.dynamic_slice_in_dim(padded_keys, row_start, window + TOK_DEV, 0).astype(jnp.float32).reshape(window + TOK_DEV, HEADS, HDIM)
        value_rows = lax.dynamic_slice_in_dim(padded_values, row_start, window + TOK_DEV, 0).astype(jnp.float32).reshape(window + TOK_DEV, HEADS, HDIM)
        query_pos = row_start + jnp.arange(TOK_DEV, dtype=jnp.int32)
        key_pos = row_start - window + jnp.arange(window + TOK_DEV, dtype=jnp.int32)
        in_window = (key_pos[None, :] <= query_pos[:, None]) & (key_pos[None, :] > query_pos[:, None] - window) & (key_pos[None, :] >= 0)
        near_scores = jnp.einsum('qhd,khd->hqk', query_rows, key_rows) * score_scale
        near_scores = jnp.where(in_window[None, :, :], near_scores, -1e+30)
        block_ids = lax.dynamic_slice_in_dim(retrieval, (block_index * per_block).astype(jnp.int32), per_block, 0)
        fetched_keys = blocks_keys[block_ids].astype(jnp.float32).reshape(per_block, TOPK * QBLK, HEADS, HDIM)
        fetched_values = blocks_values[block_ids].astype(jnp.float32).reshape(per_block, TOPK * QBLK, HEADS, HDIM)
        query_blocks = query_rows.reshape(per_block, QBLK, HEADS, HDIM)
        far_scores = jnp.einsum('bqhd,bkhd->hbqk', query_blocks, fetched_keys) * score_scale + memory_gate[:, None, None, None]
        far_scores = far_scores.reshape(HEADS, TOK_DEV, TOPK * QBLK)
        row_max = jnp.maximum(lax.optimization_barrier(jnp.max(near_scores, axis=-1)), lax.optimization_barrier(jnp.max(far_scores, axis=-1)))
        near_exp = jnp.exp(near_scores - row_max[:, :, None])
        far_exp = jnp.exp(far_scores - row_max[:, :, None])
        denominator = lax.optimization_barrier(jnp.sum(near_exp, axis=-1)) + lax.optimization_barrier(jnp.sum(far_exp, axis=-1))
        near_weights = (near_exp / denominator[:, :, None]).astype(jnp.bfloat16)
        far_weights = (far_exp / denominator[:, :, None]).astype(jnp.bfloat16)
        near_weights = lax.optimization_barrier(near_weights).astype(jnp.float32)
        far_weights = lax.optimization_barrier(far_weights).astype(jnp.float32)
        near_part = jnp.einsum('hqk,khd->qhd', near_weights, value_rows)
        far_part = jnp.einsum('hbqk,bkhd->bqhd', far_weights.reshape(HEADS, per_block, QBLK, TOPK * QBLK), fetched_values)
        combined = near_part + far_part.reshape(TOK_DEV, HEADS, HDIM)
        return combined.reshape(TOK_DEV, width).astype(jnp.bfloat16)
    result = lax.map(one_block, jnp.arange(TOKENS // TOK_DEV, dtype=jnp.int32))
    return result.reshape(TOKENS, width)
```

```python
import functools
import math

import jax
import jax.numpy as jnp
from jax import lax
from jax.experimental import pallas as pl
from jax.experimental.pallas import tpu as pltpu
from jax.sharding import PartitionSpec as P

QBLK = 64
SPAN = 4
LOW = -1e30
MESH = pl.DeviceIdType.MESH
NT = (((1,), (1,)), ((), ()))


def slot_tables(everyone, place, blocks_held, sources, capacity):
    ids = everyone.reshape(sources, -1)
    topk = everyone.shape[1]
    mine = (ids // blocks_held) == place
    rank = jnp.cumsum(mine.astype(jnp.int32), axis=1) - 1
    slots = jnp.arange(capacity, dtype=jnp.int32)
    match = mine[:, :, None] & (rank[:, :, None] == slots[None, None, :])
    entry = jnp.arange(ids.shape[1], dtype=jnp.int32)[None, :, None]
    packed = (entry // topk) * blocks_held + (ids % blocks_held)[:, :, None]
    table = jnp.sum(jnp.where(match, packed, 0), axis=1)
    count = jnp.sum(mine.astype(jnp.int32), axis=1)
    return jnp.concatenate([table, count[:, None]], axis=1)


def local_kernel(
    heads, blocks_held, capacity, place_ref, table_ref, gate_ref,
    q_ref, k_ref, v_ref, mk_ref, mv_ref, o_ref, lse_ref, acc, mref, lref,
):
    src = pl.program_id(0)
    rows = q_ref.shape[1]
    size = q_ref.shape[2] // heads
    scale = 1.0 / math.sqrt(size)
    dist = src - place_ref[0]

    def cols_of(h):
        return pl.ds(pl.multiple_of(h * size, size), size)

    def near(kind):
        tile = rows // 2

        @pl.loop(0, heads)
        def _(h):
            cols = cols_of(h)
            k = k_ref[:, cols]
            v = jnp.concatenate([v_ref[:, cols], jnp.ones((rows, size), jnp.bfloat16)], axis=1)
            for part in range(2):
                at = pl.ds(part * tile, tile)
                s = lax.dot_general(q_ref[0, at, cols], k, NT, preferred_element_type=jnp.float32) * scale
                if kind != 1:
                    qi = part * tile + lax.broadcasted_iota(jnp.int32, (tile, rows), 0)
                    ki = lax.broadcasted_iota(jnp.int32, (tile, rows), 1)
                    s = jnp.where(ki <= qi if kind == 0 else ki > qi, s, LOW)
                top = jnp.max(s, axis=1, keepdims=True)
                p = jnp.exp(s - top)
                if kind == 2:
                    p = jnp.where(ki > qi, p, 0.0)
                both = jnp.dot(p.astype(jnp.bfloat16), v, preferred_element_type=jnp.float32)
                acc[at, cols] = both[:, :size]
                lref[at, cols] = both[:, size:]
                mref[at, cols] = jnp.broadcast_to(top, (tile, size))

    @pl.when(dist == 0)
    def _():
        near(0)

    @pl.when((dist > 0) & (dist < SPAN))
    def _():
        near(1)

    @pl.when(dist == SPAN)
    def _():
        near(2)

    @pl.when((dist < 0) | (dist > SPAN))
    def _():
        acc[...] = jnp.zeros_like(acc)
        lref[...] = jnp.zeros_like(lref)
        mref[...] = jnp.full_like(mref, LOW)

    def slot(i, carry):
        packed = table_ref[src, i]
        at = pl.ds(pl.multiple_of((packed // blocks_held) * QBLK, QBLK), QBLK)
        mat = pl.ds(pl.multiple_of((packed % blocks_held) * QBLK, QBLK), QBLK)
        for h in range(heads):
            cols = slice(h * size, (h + 1) * size)
            s = lax.dot_general(q_ref[0, at, cols], mk_ref[mat, cols], NT, preferred_element_type=jnp.float32)
            s = s * scale + gate_ref[h]
            old = mref[at, cols]
            new = jnp.maximum(old, jnp.max(s, axis=1, keepdims=True))
            keep = jnp.exp(old - new)
            p = jnp.exp(s - new[:, :QBLK])
            pv = jnp.dot(p.astype(jnp.bfloat16), mv_ref[mat, cols], preferred_element_type=jnp.float32)
            acc[at, cols] = acc[at, cols] * keep + pv
            lref[at, cols] = lref[at, cols] * keep + jnp.sum(p, axis=1, keepdims=True)
            mref[at, cols] = new
        return carry

    lax.fori_loop(0, table_ref[src, capacity], slot, 0)

    step = 128

    @pl.loop(0, rows // step)
    def _(r):
        at = pl.ds(pl.multiple_of(r * step, step), step)
        lane = lax.broadcasted_iota(jnp.int32, (step, 128), 1)
        stats = jnp.full((step, 128), LOW, jnp.float32)
        for h in range(heads):
            cols = slice(h * size, (h + 1) * size)
            l = lref[at, cols]
            some = l > 0.0
            safe = jnp.where(some, l, 1.0)
            o_ref[0, at, cols] = (acc[at, cols] / safe).astype(jnp.bfloat16)
            lse = jnp.where(some, mref[at, cols] + jnp.log(safe), LOW)
            stats = jnp.where(lane == h, lse, stats)
        lse_ref[0, :, at] = stats.T[: lse_ref.shape[1]]


def partials(q_all, keys, values, mkeys, mvalues, gate, place, table, capacity):
    sources, rows, width = q_all.shape
    heads = gate.shape[0]
    stat_rows = -(-heads // 8) * 8
    whole = lambda a: pl.BlockSpec(a.shape, lambda s: (0,) * a.ndim)
    smem = pl.BlockSpec(memory_space=pltpu.SMEM)
    per = pl.BlockSpec((1, rows, width), lambda s: (s, 0, 0))
    return pl.pallas_call(
        functools.partial(local_kernel, heads, mkeys.shape[0] // QBLK, capacity),
        grid=(sources,),
        in_specs=[smem, smem, smem, per, whole(keys), whole(values), whole(mkeys), whole(mvalues)],
        out_specs=[per, pl.BlockSpec((1, stat_rows, rows), lambda s: (s, 0, 0))],
        out_shape=[
            jax.ShapeDtypeStruct(q_all.shape, jnp.bfloat16),
            jax.ShapeDtypeStruct((sources, stat_rows, rows), jnp.float32),
        ],
        scratch_shapes=[pltpu.VMEM((rows, width), jnp.float32)] * 3,
        compiler_params=pltpu.CompilerParams(vmem_limit_bytes=56 * 2**20),
    )(place, table, gate, q_all, keys, values, mkeys, mvalues)


def merge_kernel(
    heads, chips, o_hbm, lse_hbm, out_ref,
    own, own_s, twin, twin_s, left, left_s, right, right_s,
    load_sem, load_s_sem, tsend, tsend_s, trecv, trecv_s,
    usend, usend_s, urecv, urecv_s, dsend, dsend_s, drecv, drecv_s,
):
    c = lax.axis_index("ctx")
    m = lax.axis_index("mem")
    rows, width = out_ref.shape
    size = width // heads
    last = chips - 1

    barrier = pltpu.get_barrier_semaphore()
    pl.semaphore_signal(barrier, inc=1, device_id={"mem": 1 - m}, device_id_type=MESH)

    @pl.when(c > 0)
    def _():
        pl.semaphore_signal(barrier, inc=1, device_id={"ctx": c - 1}, device_id_type=MESH)

    @pl.when(c < last)
    def _():
        pl.semaphore_signal(barrier, inc=1, device_id={"ctx": c + 1}, device_id_type=MESH)

    inner = (c > 0).astype(jnp.int32) + (c < last).astype(jnp.int32)
    pl.semaphore_wait(barrier, 1 + inner)

    def remote(src, dst, ss, rs, where):
        return pltpu.make_async_remote_copy(
            src_ref=src, dst_ref=dst, send_sem=ss, recv_sem=rs, device_id=where, device_id_type=MESH
        )

    def loads(d):
        return (
            pltpu.make_async_copy(o_hbm.at[2 * d + m], own.at[d], load_sem.at[d]),
            pltpu.make_async_copy(lse_hbm.at[2 * d + m], own_s.at[d], load_s_sem.at[d]),
        )

    def twins(d):
        other = {"mem": 1 - m}
        return (
            remote(o_hbm.at[2 * d + 1 - m], twin.at[d], tsend.at[d], trecv.at[d], other),
            remote(lse_hbm.at[2 * d + 1 - m], twin_s.at[d], tsend_s.at[d], trecv_s.at[d], other),
        )

    def ups(d):
        where = {"ctx": c + 1}
        return (
            remote(own.at[d], left.at[d], usend.at[d], urecv.at[d], where),
            remote(own_s.at[d], left_s.at[d], usend_s.at[d], urecv_s.at[d], where),
        )

    def downs(d):
        where = {"ctx": c - 1}
        return (
            remote(own.at[d], right.at[d], dsend.at[d], drecv.at[d], where),
            remote(own_s.at[d], right_s.at[d], dsend_s.at[d], drecv_s.at[d], where),
        )

    order = []
    for i in range(chips):
        for d in (last - i, i):
            if d not in order:
                order.append(d)
    for d in order:
        for copy in twins(d) + loads(d):
            copy.start()

    def combine(d, into, others):
        parts = [own] + [o for o, _ in others]
        stats = [own_s[d]] + [s[d] for _, s in others]
        top = functools.reduce(jnp.maximum, stats)
        weights = [jnp.exp(s - top) for s in stats]
        total = functools.reduce(jnp.add, weights)
        own_s[d] = top + jnp.log(total)
        shares = [(w / total).T for w in weights]
        step = 64
        for r in range(rows // step):
            at = slice(r * step, (r + 1) * step)
            for h in range(heads):
                cols = slice(h * size, (h + 1) * size)
                out = None
                for part, share in zip(parts, shares):
                    term = part[d, at, cols].astype(jnp.float32) * share[at, h : h + 1]
                    out = term if out is None else out + term
                into(at, cols, out.astype(jnp.bfloat16))

    def wait_local(d):
        for copy in loads(d):
            copy.wait()
        for copy in twins(d):
            copy.wait()

    def store_own(d):
        def put(at, cols, value):
            own[d, at, cols] = value
        return put

    def store_out(at, cols, value):
        out_ref[at, cols] = value

    def visit_up(d):
        wait_local(d)

        @pl.when(c == 0)
        def _():
            combine(d, store_own(d), [(twin, twin_s)])

        @pl.when(c > 0)
        def _():
            for copy in ups(d):
                copy.wait_recv()
            combine(d, store_own(d), [(twin, twin_s), (left, left_s)])

        for copy in ups(d):
            copy.start()

    def visit_down(d):
        wait_local(d)

        @pl.when(c == last)
        def _():
            combine(d, store_own(d), [(twin, twin_s)])

        @pl.when(c < last)
        def _():
            for copy in downs(d):
                copy.wait_recv()
            combine(d, store_own(d), [(twin, twin_s), (right, right_s)])

        for copy in downs(d):
            copy.start()

    @pl.loop(0, last)
    def _(i):
        @pl.when(last - i > c)
        def _():
            visit_up(last - i)

        @pl.when(i < c)
        def _():
            visit_down(i)

    wait_local(c)

    @pl.when(c == 0)
    def _():
        for copy in downs(c):
            copy.wait_recv()
        combine(c, store_out, [(twin, twin_s), (right, right_s)])

    @pl.when(c == last)
    def _():
        for copy in ups(c):
            copy.wait_recv()
        combine(c, store_out, [(twin, twin_s), (left, left_s)])

    @pl.when((c > 0) & (c < last))
    def _():
        for copy in ups(c) + downs(c):
            copy.wait_recv()
        combine(c, store_out, [(twin, twin_s), (left, left_s), (right, right_s)])

    @pl.loop(0, chips)
    def _(d):
        @pl.when(d > c)
        def _():
            for copy in ups(d):
                copy.wait_send()

        @pl.when(d < c)
        def _():
            for copy in downs(d):
                copy.wait_send()


def merged(o, lse, heads):
    sources, rows, width = o.shape
    chips = sources // 2
    big = pltpu.VMEM((chips, rows, width), jnp.bfloat16)
    small = pltpu.VMEM((chips,) + lse.shape[1:], jnp.float32)
    return pl.pallas_call(
        functools.partial(merge_kernel, heads, chips),
        in_specs=[pl.BlockSpec(memory_space=pl.ANY)] * 2,
        out_specs=pl.BlockSpec(memory_space=pltpu.VMEM),
        out_shape=jax.ShapeDtypeStruct((rows, width), jnp.bfloat16),
        scratch_shapes=[big, small] * 4 + [pltpu.SemaphoreType.DMA((chips,))] * 14,
        compiler_params=pltpu.CompilerParams(
            collective_id=0, has_side_effects=True, vmem_limit_bytes=56 * 2**20
        ),
    )(o, lse)


def body(queries, keys, values, memory_keys, memory_values, retrieval, memory_gate):
    axes = ("ctx", "mem")
    sources = lax.axis_size(axes)
    place = lax.axis_index(axes)
    query_blocks, topk = retrieval.shape
    capacity = max(3, 3 * query_blocks * topk // (2 * sources))
    blocks_held = memory_keys.shape[0] // QBLK
    everyone = lax.all_gather(retrieval, axes, axis=0, tiled=True)
    table = slot_tables(everyone, place, blocks_held, sources, capacity)
    q_all = lax.all_gather(queries, axes, axis=0)
    o, lse = partials(
        q_all, keys, values, memory_keys, memory_values, memory_gate,
        place.reshape(1).astype(jnp.int32), table, capacity,
    )
    return merged(o, lse, memory_gate.shape[0])


def solution(mesh):
    rows = P(("groups", "ctx", "mem"), "head")
    return jax.shard_map(
        body,
        mesh=mesh,
        in_specs=(rows, rows, rows, rows, rows, P(("groups", "ctx", "mem"), None), P("head")),
        out_specs=rows,
        check_vma=False,
    )
```

```python
import functools
import math

import jax
import jax.numpy as jnp
from jax import lax
from jax.experimental import pallas as pl
from jax.experimental.pallas import tpu as pltpu
from jax.sharding import PartitionSpec as P

QBLK = 64
SPAN = 4
LOW = -1e30
LOG2E = math.log2(math.e)
MESH = pl.DeviceIdType.MESH
NT = (((1,), (1,)), ((), ()))


def slot_tables(everyone, place, blocks_held, sources, capacity):
    ids = everyone.reshape(sources, -1)
    topk = everyone.shape[1]
    mine = (ids // blocks_held) == place
    rank = jnp.cumsum(mine.astype(jnp.int32), axis=1) - 1
    slots = jnp.arange(capacity, dtype=jnp.int32)
    match = mine[:, :, None] & (rank[:, :, None] == slots[None, None, :])
    entry = jnp.arange(ids.shape[1], dtype=jnp.int32)[None, :, None]
    packed = (entry // topk) * blocks_held + (ids % blocks_held)[:, :, None]
    table = jnp.sum(jnp.where(match, packed, 0), axis=1)
    count = jnp.sum(mine.astype(jnp.int32), axis=1)
    return jnp.concatenate([table, count[:, None]], axis=1)


def local_kernel(
    heads, blocks_held, capacity, place_ref, table_ref, gate_ref,
    q_ref, k_ref, v_ref, mk_ref, mv_ref, o_ref, lse_ref, acc, mref, lref,
):
    src = pl.program_id(0)
    rows = q_ref.shape[1]
    size = q_ref.shape[2] // heads
    scale = LOG2E / math.sqrt(size)
    dist = src - place_ref[0]

    def near(kind):
        tile = rows // 2

        @pl.loop(0, heads, unroll=2)
        def _(h):
            cols = pl.ds(pl.multiple_of(h * size, size), size)
            for part in range(2):
                first, count = 0, rows
                if kind == 0 and part == 0:
                    count = tile
                if kind == 2 and part == 1:
                    first, count = tile, tile
                at = pl.ds(part * tile, tile)
                seen = pl.ds(first, count)
                s = lax.dot_general(q_ref[0, at, cols], k_ref[seen, cols], NT, preferred_element_type=jnp.float32)
                if kind != 1:
                    qi = part * tile + lax.broadcasted_iota(jnp.int32, (tile, count), 0)
                    ki = first + lax.broadcasted_iota(jnp.int32, (tile, count), 1)
                    s = jnp.where(ki <= qi if kind == 0 else ki > qi, s, LOW)
                top = jnp.max(s, axis=1, keepdims=True) * scale
                p = jnp.exp2(s * scale - top)
                if kind == 2:
                    p = jnp.where(ki > qi, p, 0.0)
                v = jnp.concatenate([v_ref[seen, cols], jnp.ones((count, size), jnp.bfloat16)], axis=1)
                both = jnp.dot(p.astype(jnp.bfloat16), v, preferred_element_type=jnp.float32)
                acc[at, cols] = both[:, :size]
                lref[at, cols] = both[:, size:]
                mref[at, cols] = jnp.broadcast_to(jnp.maximum(top, LOW), (tile, size))

    @pl.when(dist == 0)
    def _():
        near(0)

    @pl.when((dist > 0) & (dist < SPAN))
    def _():
        near(1)

    @pl.when(dist == SPAN)
    def _():
        near(2)

    @pl.when((dist < 0) | (dist > SPAN))
    def _():
        acc[...] = jnp.zeros_like(acc)
        lref[...] = jnp.zeros_like(lref)
        mref[...] = jnp.full_like(mref, LOW)

    number = table_ref[src, capacity]

    def slots(i, carry):
        work = []
        for j in range(2):
            at_slot = 2 * i + j
            packed = table_ref[src, at_slot]
            at = pl.ds(pl.multiple_of((packed // blocks_held) * QBLK, QBLK), QBLK)
            mat = pl.ds(pl.multiple_of((packed % blocks_held) * QBLK, QBLK), QBLK)
            for h in range(heads):
                work.append((at, mat, slice(h * size, (h + 1) * size), h, at_slot < number))
        raw = [
            lax.dot_general(q_ref[0, at, cols], mk_ref[mat, cols], NT, preferred_element_type=jnp.float32)
            for at, mat, cols, h, real in work
        ]
        raw = [
            jnp.where(real, s * scale + gate_ref[h] * LOG2E, 2 * LOW)
            for s, (at, mat, cols, h, real) in zip(raw, work)
        ]
        tops = [jnp.max(s, axis=1, keepdims=True) for s in raw]
        probs = [jnp.exp2(s - top).astype(jnp.bfloat16) for s, top in zip(raw, tops)]
        ones = jnp.ones((QBLK, size), jnp.bfloat16)
        sums = [
            jnp.dot(p, jnp.concatenate([mv_ref[mat, cols], ones], axis=1), preferred_element_type=jnp.float32)
            for p, (at, mat, cols, h, real) in zip(probs, work)
        ]
        for top, both, (at, mat, cols, h, real) in zip(tops, sums, work):
            old = mref[at, cols]
            new = jnp.maximum(old, top)
            keep = jnp.exp2(old - new)
            add = jnp.exp2(top - new)
            acc[at, cols] = acc[at, cols] * keep + both[:, :size] * add
            lref[at, cols] = lref[at, cols] * keep + both[:, size:] * add
            mref[at, cols] = new
        return carry

    lax.fori_loop(0, (number + 1) // 2, slots, 0)

    step = 128

    @pl.loop(0, rows // step)
    def _(r):
        at = pl.ds(pl.multiple_of(r * step, step), step)
        lane = lax.broadcasted_iota(jnp.int32, (step, 128), 1)
        tops = jnp.full((step, 128), LOW, jnp.float32)
        sums = jnp.ones((step, 128), jnp.float32)
        for h in range(heads):
            cols = slice(h * size, (h + 1) * size)
            l = lref[at, cols]
            safe = jnp.where(l > 0.0, l, 1.0)
            o_ref[0, at, cols] = (acc[at, cols] / safe).astype(jnp.bfloat16)
            tops = jnp.where(lane == h, mref[at, cols], tops)
            sums = jnp.where(lane == h, safe, sums)
        lse_ref[0, :, at] = (tops + jnp.log2(sums)).T[: lse_ref.shape[1]]


def partials(q_all, keys, values, mkeys, mvalues, gate, place, table, capacity, group):
    sources, rows, width = q_all.shape
    heads = gate.shape[0]
    stat_rows = -(-heads // 8) * 8
    side = lambda a: pl.BlockSpec((a.shape[0], width), lambda s: (0, group))
    smem = pl.BlockSpec(memory_space=pltpu.SMEM)
    per = pl.BlockSpec((1, rows, width), lambda s: (s, 0, 0))
    return pl.pallas_call(
        functools.partial(local_kernel, heads, mkeys.shape[0] // QBLK, capacity),
        grid=(sources,),
        in_specs=[smem, smem, smem, per, side(keys), side(values), side(mkeys), side(mvalues)],
        out_specs=[per, pl.BlockSpec((1, stat_rows, rows), lambda s: (s, 0, 0))],
        out_shape=[
            jax.ShapeDtypeStruct(q_all.shape, jnp.bfloat16),
            jax.ShapeDtypeStruct((sources, stat_rows, rows), jnp.float32),
        ],
        scratch_shapes=[pltpu.VMEM((rows, width), jnp.float32)] * 3,
        compiler_params=pltpu.CompilerParams(vmem_limit_bytes=56 * 2**20),
        cost_estimate=pl.CostEstimate(
            flops=20 * rows * rows * width, bytes_accessed=64 * rows * width, transcendentals=rows * rows * heads
        ),
    )(place, table, gate, q_all, keys, values, mkeys, mvalues)


def merge_kernel(
    heads, chips, halves, o_a, lse_a, o_b, lse_b, out_ref,
    own, own_s, twin, twin_s, left, left_s, right, right_s,
    load_sem, load_s_sem, tsend, tsend_s, trecv, trecv_s,
    usend, usend_s, urecv, urecv_s, dsend, dsend_s, drecv, drecv_s,
):
    c = lax.axis_index("ctx")
    m = lax.axis_index("mem")
    rows, width = out_ref.shape
    size = width // heads
    half = rows // halves
    wide = width // 2
    last = chips - 1
    hbm = ((o_a, lse_a), (o_b, lse_b))

    barrier = pltpu.get_barrier_semaphore()
    pl.semaphore_signal(barrier, inc=1, device_id={"mem": 1 - m}, device_id_type=MESH)

    @pl.when(c > 0)
    def _():
        pl.semaphore_signal(barrier, inc=1, device_id={"ctx": c - 1}, device_id_type=MESH)

    @pl.when(c < last)
    def _():
        pl.semaphore_signal(barrier, inc=1, device_id={"ctx": c + 1}, device_id_type=MESH)

    inner = (c > 0).astype(jnp.int32) + (c < last).astype(jnp.int32)
    pl.semaphore_wait(barrier, 1 + inner)

    def remote(src, dst, ss, rs, where):
        return pltpu.make_async_remote_copy(
            src_ref=src, dst_ref=dst, send_sem=ss, recv_sem=rs, device_id=where, device_id_type=MESH
        )

    def spots(g, d, r):
        at = pl.ds(pl.multiple_of(r * half, half), half)
        return (g, d, at), (g, d, slice(None), at), (at, (slice(None), at)), (g * chips + d) * halves + r

    def loads(g, d, r):
        big, small, (at, at_s), n = spots(g, d, r)
        o_hbm, lse_hbm = hbm[g]
        return (
            pltpu.make_async_copy(o_hbm.at[2 * d + m, at], own.at[big], load_sem.at[n]),
            pltpu.make_async_copy(lse_hbm.at[2 * d + m, :, at], own_s.at[small], load_s_sem.at[n]),
        )

    def twins(g, d, r):
        big, small, (at, at_s), n = spots(g, d, r)
        o_hbm, lse_hbm = hbm[g]
        other = {"mem": 1 - m}
        return (
            remote(o_hbm.at[2 * d + 1 - m, at], twin.at[big], tsend.at[n], trecv.at[n], other),
            remote(lse_hbm.at[2 * d + 1 - m, :, at], twin_s.at[small], tsend_s.at[n], trecv_s.at[n], other),
        )

    def ups(g, d, r):
        big, small, _, n = spots(g, d, r)
        where = {"ctx": c + 1}
        return (
            remote(own.at[big], left.at[big], usend.at[n], urecv.at[n], where),
            remote(own_s.at[small], left_s.at[small], usend_s.at[n], urecv_s.at[n], where),
        )

    def downs(g, d, r):
        big, small, _, n = spots(g, d, r)
        where = {"ctx": c - 1}
        return (
            remote(own.at[big], right.at[big], dsend.at[n], drecv.at[n], where),
            remote(own_s.at[small], right_s.at[small], dsend_s.at[n], drecv_s.at[n], where),
        )

    order = []
    for i in range(chips):
        for d in (last - i, i):
            if d not in order:
                order.append(d)
    for d in order:
        for g in range(2):
            @pl.loop(0, halves)
            def _(r):
                for copy in twins(g, d, r) + loads(g, d, r):
                    copy.start()

    def combine(g, d, r, into, others):
        big, small, _, _ = spots(g, d, r)
        parts = [own] + [o for o, _ in others]
        stats = [own_s[small]] + [s[small] for _, s in others]
        top = functools.reduce(jnp.maximum, stats)
        weights = [jnp.exp2(s - top) for s in stats]
        total = functools.reduce(jnp.add, weights)
        own_s[small] = top + jnp.log2(total)
        shares = [(w / total).T for w in weights]
        step = 64
        for t in range(half // step):
            at = pl.ds(pl.multiple_of(r * half + t * step, step), step)
            for h in range(heads // 2):
                cols = slice(h * size, (h + 1) * size)
                out = None
                for part, share in zip(parts, shares):
                    term = part[g, d, at, cols].astype(jnp.float32) * share[t * step : (t + 1) * step, h : h + 1]
                    out = term if out is None else out + term
                into(at, cols, out.astype(jnp.bfloat16))

    def wait_local(g, d, r):
        for copy in loads(g, d, r):
            copy.wait()
        for copy in twins(g, d, r):
            copy.wait()

    def store_own(g, d):
        def put(at, cols, value):
            own[g, d, at, cols] = value
        return put

    def store_out(g):
        def put(at, cols, value):
            out_ref[at, g * wide + cols.start : g * wide + cols.stop] = value
        return put

    def visit(g, d, r, copies, first, arrived):
        wait_local(g, d, r)

        @pl.when(first)
        def _():
            combine(g, d, r, store_own(g, d), [(twin, twin_s)])

        @pl.when(jnp.logical_not(first))
        def _():
            for copy in copies(g, d, r):
                copy.wait_recv()
            combine(g, d, r, store_own(g, d), [(twin, twin_s), arrived])

        for copy in copies(g, d, r):
            copy.start()

    @pl.loop(0, last)
    def _(i):
        for g in range(2):
            @pl.loop(0, halves)
            def _(r):
                @pl.when(last - i > c)
                def _():
                    visit(g, last - i, r, ups, c == 0, (left, left_s))

                @pl.when(i < c)
                def _():
                    visit(g, i, r, downs, c == last, (right, right_s))

    for g in range(2):
        @pl.loop(0, halves)
        def _(r):
            wait_local(g, c, r)

            @pl.when(c == 0)
            def _():
                for copy in downs(g, c, r):
                    copy.wait_recv()
                combine(g, c, r, store_out(g), [(twin, twin_s), (right, right_s)])

            @pl.when(c == last)
            def _():
                for copy in ups(g, c, r):
                    copy.wait_recv()
                combine(g, c, r, store_out(g), [(twin, twin_s), (left, left_s)])

            @pl.when((c > 0) & (c < last))
            def _():
                for copy in ups(g, c, r) + downs(g, c, r):
                    copy.wait_recv()
                combine(g, c, r, store_out(g), [(twin, twin_s), (left, left_s), (right, right_s)])

    @pl.loop(0, chips)
    def _(d):
        for g in range(2):
            @pl.loop(0, halves)
            def _(r):
                @pl.when(d > c)
                def _():
                    for copy in ups(g, d, r):
                        copy.wait_send()

                @pl.when(d < c)
                def _():
                    for copy in downs(g, d, r):
                        copy.wait_send()


def merged(first, second, heads):
    (o_a, lse_a), (o_b, lse_b) = first, second
    sources, rows, width = o_a.shape
    chips = sources // 2
    halves = 2 if chips <= 4 else 1
    big = pltpu.VMEM((2, chips, rows, width), jnp.bfloat16)
    small = pltpu.VMEM((2, chips) + lse_a.shape[1:], jnp.float32)
    return pl.pallas_call(
        functools.partial(merge_kernel, heads, chips, halves),
        in_specs=[pl.BlockSpec(memory_space=pl.ANY)] * 4,
        out_specs=pl.BlockSpec(memory_space=pltpu.VMEM),
        out_shape=jax.ShapeDtypeStruct((rows, 2 * width), jnp.bfloat16),
        scratch_shapes=[big, small] * 4 + [pltpu.SemaphoreType.DMA((2 * chips * halves,))] * 14,
        compiler_params=pltpu.CompilerParams(
            collective_id=0, has_side_effects=True, vmem_limit_bytes=56 * 2**20
        ),
    )(o_a, lse_a, o_b, lse_b)


def body(queries, keys, values, memory_keys, memory_values, retrieval, memory_gate):
    axes = ("ctx", "mem")
    sources = lax.axis_size(axes)
    place = lax.axis_index(axes)
    query_blocks, topk = retrieval.shape
    capacity = max(3, 3 * query_blocks * topk // (2 * sources))
    blocks_held = memory_keys.shape[0] // QBLK
    heads = memory_gate.shape[0]
    wide = queries.shape[1] // 2
    everyone = lax.all_gather(retrieval, axes, axis=0, tiled=True)
    table = slot_tables(everyone, place, blocks_held, sources, capacity)
    q_a = lax.all_gather(queries[:, :wide], axes, axis=0)
    later, q_a, table = lax.optimization_barrier((queries[:, wide:], q_a, table))
    q_b = lax.all_gather(later, axes, axis=0)
    where = place.reshape(1).astype(jnp.int32)
    sides = (keys, values, memory_keys, memory_values)
    first = partials(q_a, *sides, memory_gate[: heads // 2], where, table, capacity, 0)
    second = partials(q_b, *sides, memory_gate[heads // 2 :], where, table, capacity, 1)
    return merged(first, second, heads)


def solution(mesh):
    rows = P(("groups", "ctx", "mem"), "head")
    return jax.shard_map(
        body,
        mesh=mesh,
        in_specs=(rows, rows, rows, rows, rows, P(("groups", "ctx", "mem"), None), P("head")),
        out_specs=rows,
        check_vma=False,
    )
```

```python
import functools
import math

import jax
import jax.numpy as jnp
from jax import lax
from jax.experimental import pallas as pl
from jax.experimental.pallas import tpu as pltpu
from jax.sharding import PartitionSpec as P

QBLK = 64
SPAN = 4
LOW = -1e30
LOG2E = math.log2(math.e)
MESH = pl.DeviceIdType.MESH
NT = (((1,), (1,)), ((), ()))


def slot_tables(everyone, place, blocks_held, sources, capacity):
    ids = everyone.reshape(sources, -1)
    topk = everyone.shape[1]
    mine = (ids // blocks_held) == place
    rank = jnp.cumsum(mine.astype(jnp.int32), axis=1) - 1
    slots = jnp.arange(capacity, dtype=jnp.int32)
    match = mine[:, :, None] & (rank[:, :, None] == slots[None, None, :])
    entry = jnp.arange(ids.shape[1], dtype=jnp.int32)[None, :, None]
    packed = (entry // topk) * blocks_held + (ids % blocks_held)[:, :, None]
    table = jnp.sum(jnp.where(match, packed, 0), axis=1)
    count = jnp.sum(mine.astype(jnp.int32), axis=1)
    return jnp.concatenate([table, count[:, None]], axis=1)


def local_kernel(
    heads, blocks_held, capacity, place_ref, table_ref, gate_ref,
    q_ref, k_ref, v_ref, mk_ref, mv_ref, o_ref, lse_ref, acc, mref, lref,
):
    src = pl.program_id(0)
    rows = q_ref.shape[1]
    size = q_ref.shape[2] // heads
    scale = LOG2E / math.sqrt(size)
    dist = src - place_ref[0]

    def near(kind):
        tile = rows // 2

        @pl.loop(0, heads, unroll=2)
        def _(h):
            cols = pl.ds(pl.multiple_of(h * size, size), size)
            for part in range(2):
                first, count = 0, rows
                if kind == 0 and part == 0:
                    count = tile
                if kind == 2 and part == 1:
                    first, count = tile, tile
                at = pl.ds(part * tile, tile)
                seen = pl.ds(first, count)
                s = lax.dot_general(q_ref[0, at, cols], k_ref[seen, cols], NT, preferred_element_type=jnp.float32)
                if kind != 1:
                    qi = part * tile + lax.broadcasted_iota(jnp.int32, (tile, count), 0)
                    ki = first + lax.broadcasted_iota(jnp.int32, (tile, count), 1)
                    s = jnp.where(ki <= qi if kind == 0 else ki > qi, s, LOW)
                top = jnp.max(s, axis=1, keepdims=True) * scale
                p = jnp.exp2(s * scale - top)
                if kind == 2:
                    p = jnp.where(ki > qi, p, 0.0)
                v = jnp.concatenate([v_ref[seen, cols], jnp.ones((count, size), jnp.bfloat16)], axis=1)
                both = jnp.dot(p.astype(jnp.bfloat16), v, preferred_element_type=jnp.float32)
                acc[at, cols] = both[:, :size]
                lref[at, cols] = both[:, size:]
                mref[at, cols] = jnp.broadcast_to(jnp.maximum(top, LOW), (tile, size))

    @pl.when(dist == 0)
    def _():
        near(0)

    @pl.when((dist > 0) & (dist < SPAN))
    def _():
        near(1)

    @pl.when(dist == SPAN)
    def _():
        near(2)

    @pl.when((dist < 0) | (dist > SPAN))
    def _():
        acc[...] = jnp.zeros_like(acc)
        lref[...] = jnp.zeros_like(lref)
        mref[...] = jnp.full_like(mref, LOW)

    number = table_ref[src, capacity]

    def slots(i, carry):
        work = []
        for j in range(2):
            at_slot = 2 * i + j
            packed = table_ref[src, at_slot]
            at = pl.ds(pl.multiple_of((packed // blocks_held) * QBLK, QBLK), QBLK)
            mat = pl.ds(pl.multiple_of((packed % blocks_held) * QBLK, QBLK), QBLK)
            for h in range(heads):
                work.append((at, mat, slice(h * size, (h + 1) * size), h, at_slot < number))
        raw = [
            lax.dot_general(q_ref[0, at, cols], mk_ref[mat, cols], NT, preferred_element_type=jnp.float32)
            for at, mat, cols, h, real in work
        ]
        raw = [
            jnp.where(real, s * scale + gate_ref[h] * LOG2E, 2 * LOW)
            for s, (at, mat, cols, h, real) in zip(raw, work)
        ]
        tops = [jnp.max(s, axis=1, keepdims=True) for s in raw]
        probs = [jnp.exp2(s - top).astype(jnp.bfloat16) for s, top in zip(raw, tops)]
        ones = jnp.ones((QBLK, size), jnp.bfloat16)
        sums = [
            jnp.dot(p, jnp.concatenate([mv_ref[mat, cols], ones], axis=1), preferred_element_type=jnp.float32)
            for p, (at, mat, cols, h, real) in zip(probs, work)
        ]
        for top, both, (at, mat, cols, h, real) in zip(tops, sums, work):
            old = mref[at, cols]
            new = jnp.maximum(old, top)
            keep = jnp.exp2(old - new)
            add = jnp.exp2(top - new)
            acc[at, cols] = acc[at, cols] * keep + both[:, :size] * add
            lref[at, cols] = lref[at, cols] * keep + both[:, size:] * add
            mref[at, cols] = new
        return carry

    lax.fori_loop(0, (number + 1) // 2, slots, 0)

    step = 128

    @pl.loop(0, rows // step)
    def _(r):
        at = pl.ds(pl.multiple_of(r * step, step), step)
        lane = lax.broadcasted_iota(jnp.int32, (step, 128), 1)
        tops = jnp.full((step, 128), LOW, jnp.float32)
        sums = jnp.ones((step, 128), jnp.float32)
        for h in range(heads):
            cols = slice(h * size, (h + 1) * size)
            l = lref[at, cols]
            safe = jnp.where(l > 0.0, l, 1.0)
            o_ref[0, at, cols] = (acc[at, cols] / safe).astype(jnp.bfloat16)
            tops = jnp.where(lane == h, mref[at, cols], tops)
            sums = jnp.where(lane == h, safe, sums)
        lse_ref[0, :, at] = (tops + jnp.log2(sums)).T[: lse_ref.shape[1]]


def partials(q_all, keys, values, mkeys, mvalues, gate, place, table, capacity, group):
    sources, _, width = q_all.shape
    rows = keys.shape[0]
    heads = gate.shape[0]
    stat_rows = -(-heads // 8) * 8
    side = lambda a: pl.BlockSpec((a.shape[0], width), lambda s: (0, group))
    smem = pl.BlockSpec(memory_space=pltpu.SMEM)
    per = pl.BlockSpec((1, rows, width), lambda s: (s, 0, 0))
    return pl.pallas_call(
        functools.partial(local_kernel, heads, mkeys.shape[0] // QBLK, capacity),
        grid=(sources,),
        in_specs=[smem, smem, smem, per, side(keys), side(values), side(mkeys), side(mvalues)],
        out_specs=[per, pl.BlockSpec((1, stat_rows, rows), lambda s: (s, 0, 0))],
        out_shape=[
            jax.ShapeDtypeStruct((sources, rows, width), jnp.bfloat16),
            jax.ShapeDtypeStruct((sources, stat_rows, rows), jnp.float32),
        ],
        scratch_shapes=[pltpu.VMEM((rows, width), jnp.float32)] * 3,
        compiler_params=pltpu.CompilerParams(vmem_limit_bytes=56 * 2**20),
        cost_estimate=pl.CostEstimate(
            flops=20 * rows * rows * width, bytes_accessed=64 * rows * width, transcendentals=rows * rows * heads
        ),
    )(place, table, gate, q_all, keys, values, mkeys, mvalues)


def merge_kernel(
    heads, chips, halves, o_a, lse_a, o_b, lse_b, out_ref,
    own, own_s, twin, twin_s, left, left_s, right, right_s,
    load_sem, load_s_sem, tsend, tsend_s, trecv, trecv_s,
    usend, usend_s, urecv, urecv_s, dsend, dsend_s, drecv, drecv_s,
):
    c = lax.axis_index("ctx")
    m = lax.axis_index("mem")
    rows, width = out_ref.shape
    size = width // heads
    half = rows // halves
    wide = width // 2
    last = chips - 1
    hbm = ((o_a, lse_a), (o_b, lse_b))

    barrier = pltpu.get_barrier_semaphore()
    pl.semaphore_signal(barrier, inc=1, device_id={"mem": 1 - m}, device_id_type=MESH)

    @pl.when(c > 0)
    def _():
        pl.semaphore_signal(barrier, inc=1, device_id={"ctx": c - 1}, device_id_type=MESH)

    @pl.when(c < last)
    def _():
        pl.semaphore_signal(barrier, inc=1, device_id={"ctx": c + 1}, device_id_type=MESH)

    inner = (c > 0).astype(jnp.int32) + (c < last).astype(jnp.int32)
    pl.semaphore_wait(barrier, 1 + inner)

    def remote(src, dst, ss, rs, where):
        return pltpu.make_async_remote_copy(
            src_ref=src, dst_ref=dst, send_sem=ss, recv_sem=rs, device_id=where, device_id_type=MESH
        )

    def spots(g, d, r):
        at = pl.ds(pl.multiple_of(r * half, half), half)
        return (g, d, at), (g, d, slice(None), at), (at, (slice(None), at)), (g * chips + d) * halves + r

    def loads(g, d, r):
        big, small, (at, at_s), n = spots(g, d, r)
        o_hbm, lse_hbm = hbm[g]
        return (
            pltpu.make_async_copy(o_hbm.at[2 * d + m, at], own.at[big], load_sem.at[n]),
            pltpu.make_async_copy(lse_hbm.at[2 * d + m, :, at], own_s.at[small], load_s_sem.at[n]),
        )

    def twins(g, d, r):
        big, small, (at, at_s), n = spots(g, d, r)
        o_hbm, lse_hbm = hbm[g]
        other = {"mem": 1 - m}
        return (
            remote(o_hbm.at[2 * d + 1 - m, at], twin.at[big], tsend.at[n], trecv.at[n], other),
            remote(lse_hbm.at[2 * d + 1 - m, :, at], twin_s.at[small], tsend_s.at[n], trecv_s.at[n], other),
        )

    def ups(g, d, r):
        big, small, _, n = spots(g, d, r)
        where = {"ctx": c + 1}
        return (
            remote(own.at[big], left.at[big], usend.at[n], urecv.at[n], where),
            remote(own_s.at[small], left_s.at[small], usend_s.at[n], urecv_s.at[n], where),
        )

    def downs(g, d, r):
        big, small, _, n = spots(g, d, r)
        where = {"ctx": c - 1}
        return (
            remote(own.at[big], right.at[big], dsend.at[n], drecv.at[n], where),
            remote(own_s.at[small], right_s.at[small], dsend_s.at[n], drecv_s.at[n], where),
        )

    order = []
    for i in range(chips):
        for d in (last - i, i):
            if d not in order:
                order.append(d)
    for d in order:
        for g in range(2):
            @pl.loop(0, halves)
            def _(r):
                for copy in twins(g, d, r) + loads(g, d, r):
                    copy.start()

    def combine(g, d, r, into, others):
        big, small, _, _ = spots(g, d, r)
        parts = [own] + [o for o, _ in others]
        stats = [own_s[small]] + [s[small] for _, s in others]
        top = functools.reduce(jnp.maximum, stats)
        weights = [jnp.exp2(s - top) for s in stats]
        total = functools.reduce(jnp.add, weights)
        own_s[small] = top + jnp.log2(total)
        shares = [(w / total).T for w in weights]
        step = 64
        for t in range(half // step):
            at = pl.ds(pl.multiple_of(r * half + t * step, step), step)
            for h in range(heads // 2):
                cols = slice(h * size, (h + 1) * size)
                out = None
                for part, share in zip(parts, shares):
                    term = part[g, d, at, cols].astype(jnp.float32) * share[t * step : (t + 1) * step, h : h + 1]
                    out = term if out is None else out + term
                into(at, cols, out.astype(jnp.bfloat16))

    def wait_local(g, d, r):
        for copy in loads(g, d, r):
            copy.wait()
        for copy in twins(g, d, r):
            copy.wait()

    def store_own(g, d):
        def put(at, cols, value):
            own[g, d, at, cols] = value
        return put

    def store_out(g):
        def put(at, cols, value):
            out_ref[at, g * wide + cols.start : g * wide + cols.stop] = value
        return put

    def visit(g, d, r, copies, first, arrived):
        wait_local(g, d, r)

        @pl.when(first)
        def _():
            combine(g, d, r, store_own(g, d), [(twin, twin_s)])

        @pl.when(jnp.logical_not(first))
        def _():
            for copy in copies(g, d, r):
                copy.wait_recv()
            combine(g, d, r, store_own(g, d), [(twin, twin_s), arrived])

        for copy in copies(g, d, r):
            copy.start()

    @pl.loop(0, last)
    def _(i):
        for g in range(2):
            @pl.loop(0, halves)
            def _(r):
                @pl.when(last - i > c)
                def _():
                    visit(g, last - i, r, ups, c == 0, (left, left_s))

                @pl.when(i < c)
                def _():
                    visit(g, i, r, downs, c == last, (right, right_s))

    for g in range(2):
        @pl.loop(0, halves)
        def _(r):
            wait_local(g, c, r)

            @pl.when(c == 0)
            def _():
                for copy in downs(g, c, r):
                    copy.wait_recv()
                combine(g, c, r, store_out(g), [(twin, twin_s), (right, right_s)])

            @pl.when(c == last)
            def _():
                for copy in ups(g, c, r):
                    copy.wait_recv()
                combine(g, c, r, store_out(g), [(twin, twin_s), (left, left_s)])

            @pl.when((c > 0) & (c < last))
            def _():
                for copy in ups(g, c, r) + downs(g, c, r):
                    copy.wait_recv()
                combine(g, c, r, store_out(g), [(twin, twin_s), (left, left_s), (right, right_s)])

    @pl.loop(0, chips)
    def _(d):
        for g in range(2):
            @pl.loop(0, halves)
            def _(r):
                @pl.when(d > c)
                def _():
                    for copy in ups(g, d, r):
                        copy.wait_send()

                @pl.when(d < c)
                def _():
                    for copy in downs(g, d, r):
                        copy.wait_send()


def merged(first, second, heads):
    (o_a, lse_a), (o_b, lse_b) = first, second
    sources, rows, width = o_a.shape
    chips = sources // 2
    halves = 2 if chips <= 4 else 1
    big = pltpu.VMEM((2, chips, rows, width), jnp.bfloat16)
    small = pltpu.VMEM((2, chips) + lse_a.shape[1:], jnp.float32)
    return pl.pallas_call(
        functools.partial(merge_kernel, heads, chips, halves),
        in_specs=[pl.BlockSpec(memory_space=pl.ANY)] * 4,
        out_specs=pl.BlockSpec(memory_space=pltpu.VMEM),
        out_shape=jax.ShapeDtypeStruct((rows, 2 * width), jnp.bfloat16),
        scratch_shapes=[big, small] * 4 + [pltpu.SemaphoreType.DMA((2 * chips * halves,))] * 14,
        compiler_params=pltpu.CompilerParams(
            collective_id=0, has_side_effects=True, vmem_limit_bytes=56 * 2**20
        ),
    )(o_a, lse_a, o_b, lse_b)


def gather_kernel(chips, q_ref, out_ref, own_sem, usend, urecv, dsend, drecv, tsend, trecv):
    c = lax.axis_index("ctx")
    m = lax.axis_index("mem")
    last = chips - 1
    barrier = pltpu.get_barrier_semaphore()
    pl.semaphore_signal(barrier, inc=1, device_id={"mem": 1 - m}, device_id_type=MESH)

    @pl.when(c > 0)
    def _():
        pl.semaphore_signal(barrier, inc=1, device_id={"ctx": c - 1}, device_id_type=MESH)

    @pl.when(c < last)
    def _():
        pl.semaphore_signal(barrier, inc=1, device_id={"ctx": c + 1}, device_id_type=MESH)

    inner = (c > 0).astype(jnp.int32) + (c < last).astype(jnp.int32)
    pl.semaphore_wait(barrier, 1 + inner)

    def copy(src, d, sends, recvs, where):
        return pltpu.make_async_remote_copy(
            src_ref=src, dst_ref=out_ref.at[2 * d + m], send_sem=sends.at[d], recv_sem=recvs.at[d],
            device_id=where, device_id_type=MESH,
        )

    def up(src, d):
        return copy(src, d, usend, urecv, {"ctx": c + 1})

    def down(src, d):
        return copy(src, d, dsend, drecv, {"ctx": c - 1})

    def twin(src, d):
        return copy(src, d, tsend, trecv, {"mem": 1 - m})

    @pl.when(c < last)
    def _():
        up(q_ref, c).start()

    @pl.when(c > 0)
    def _():
        down(q_ref, c).start()

    twin(q_ref, c).start()
    own = pltpu.make_async_copy(q_ref, out_ref.at[2 * c + m], own_sem)
    own.start()

    @pl.loop(0, last)
    def _(t):
        low = c - 1 - t
        high = c + 1 + t

        @pl.when(low >= 0)
        def _():
            block = out_ref.at[2 * low + m]
            up(block, low).wait_recv()

            @pl.when(c < last)
            def _():
                up(block, low).start()

            twin(block, low).start()

        @pl.when(high <= last)
        def _():
            block = out_ref.at[2 * high + m]
            down(block, high).wait_recv()

            @pl.when(c > 0)
            def _():
                down(block, high).start()

            twin(block, high).start()

    own.wait()

    @pl.loop(0, chips)
    def _(d):
        twin(q_ref, d).wait()

        @pl.when((d <= c) & (c < last))
        def _():
            up(q_ref, d).wait_send()

        @pl.when((d >= c) & (c > 0))
        def _():
            down(q_ref, d).wait_send()


def gathered(q, sources):
    chips = sources // 2
    return pl.pallas_call(
        functools.partial(gather_kernel, chips),
        in_specs=[pl.BlockSpec(memory_space=pl.ANY)],
        out_specs=pl.BlockSpec(memory_space=pl.ANY),
        out_shape=jax.ShapeDtypeStruct((sources,) + q.shape, q.dtype),
        scratch_shapes=[pltpu.SemaphoreType.DMA] + [pltpu.SemaphoreType.DMA((chips,))] * 6,
        compiler_params=pltpu.CompilerParams(collective_id=1, has_side_effects=True),
    )(q)


def body(queries, keys, values, memory_keys, memory_values, retrieval, memory_gate):
    axes = ("ctx", "mem")
    sources = lax.axis_size(axes)
    place = lax.axis_index(axes)
    query_blocks, topk = retrieval.shape
    capacity = max(3, 3 * query_blocks * topk // (2 * sources))
    blocks_held = memory_keys.shape[0] // QBLK
    heads = memory_gate.shape[0]
    wide = queries.shape[1] // 2
    tok_rows = queries.shape[0]
    ids = retrieval.reshape(1, -1)
    halves = jnp.concatenate([ids // 256, ids % 256], axis=0).astype(queries.dtype)
    tail = jnp.pad(halves, ((0, 14), (0, wide - ids.shape[1])))
    q_a = gathered(jnp.concatenate([queries[:, :wide], tail], axis=0), sources)
    later, q_a = lax.optimization_barrier((queries[:, wide:], q_a))
    q_b = lax.all_gather(later, axes, axis=0)
    got = q_a[:, tok_rows : tok_rows + 2, : ids.shape[1]].astype(jnp.int32)
    everyone = (got[:, 0] * 256 + got[:, 1]).reshape(-1, topk)
    table = slot_tables(everyone, place, blocks_held, sources, capacity)
    where = place.reshape(1).astype(jnp.int32)
    sides = (keys, values, memory_keys, memory_values)
    first = partials(q_a, *sides, memory_gate[: heads // 2], where, table, capacity, 0)
    second = partials(q_b, *sides, memory_gate[heads // 2 :], where, table, capacity, 1)
    return merged(first, second, heads)


def solution(mesh):
    rows = P(("groups", "ctx", "mem"), "head")
    return jax.shard_map(
        body,
        mesh=mesh,
        in_specs=(rows, rows, rows, rows, rows, P(("groups", "ctx", "mem"), None), P("head")),
        out_specs=rows,
        check_vma=False,
    )
```

```python
import functools
import math

import jax
import jax.numpy as jnp
from jax import lax
from jax.experimental import pallas as pl
from jax.experimental.pallas import tpu as pltpu
from jax.sharding import PartitionSpec as P

QBLK = 64
SPAN = 4
LOW = -1e30
LOG2E = math.log2(math.e)
MESH = pl.DeviceIdType.MESH
NT = (((1,), (1,)), ((), ()))


def slot_tables(everyone, place, blocks_held, sources, capacity):
    ids = everyone.reshape(sources, -1)
    topk = everyone.shape[1]
    mine = (ids // blocks_held) == place
    rank = jnp.cumsum(mine.astype(jnp.int32), axis=1) - 1
    slots = jnp.arange(capacity, dtype=jnp.int32)
    match = mine[:, :, None] & (rank[:, :, None] == slots[None, None, :])
    entry = jnp.arange(ids.shape[1], dtype=jnp.int32)[None, :, None]
    packed = (entry // topk) * blocks_held + (ids % blocks_held)[:, :, None]
    table = jnp.sum(jnp.where(match, packed, 0), axis=1)
    count = jnp.sum(mine.astype(jnp.int32), axis=1)
    return jnp.concatenate([table, count[:, None]], axis=1)


def local_kernel(
    heads, blocks_held, capacity, place_ref, table_ref, gate_ref,
    q_ref, k_ref, v_ref, mk_ref, mv_ref, o_ref, lse_ref, acc, mref, lref,
):
    src = pl.program_id(0)
    rows = q_ref.shape[1]
    size = q_ref.shape[2] // heads
    scale = LOG2E / math.sqrt(size)
    dist = src - place_ref[0]

    def near(kind):
        tile = rows // 2

        @pl.loop(0, heads, unroll=2)
        def _(h):
            cols = pl.ds(pl.multiple_of(h * size, size), size)
            for part in range(2):
                first, count = 0, rows
                if kind == 0 and part == 0:
                    count = tile
                if kind == 2 and part == 1:
                    first, count = tile, tile
                at = pl.ds(part * tile, tile)
                seen = pl.ds(first, count)
                s = lax.dot_general(q_ref[0, at, cols], k_ref[seen, cols], NT, preferred_element_type=jnp.float32)
                if kind != 1:
                    qi = part * tile + lax.broadcasted_iota(jnp.int32, (tile, count), 0)
                    ki = first + lax.broadcasted_iota(jnp.int32, (tile, count), 1)
                    s = jnp.where(ki <= qi if kind == 0 else ki > qi, s, LOW)
                top = jnp.max(s, axis=1, keepdims=True) * scale
                p = jnp.exp2(s * scale - top)
                if kind == 2:
                    p = jnp.where(ki > qi, p, 0.0)
                v = jnp.concatenate([v_ref[seen, cols], jnp.ones((count, size), jnp.bfloat16)], axis=1)
                both = jnp.dot(p.astype(jnp.bfloat16), v, preferred_element_type=jnp.float32)
                acc[at, cols] = both[:, :size]
                lref[at, cols] = both[:, size:]
                mref[at, cols] = jnp.broadcast_to(jnp.maximum(top, LOW), (tile, size))

    @pl.when(dist == 0)
    def _():
        near(0)

    @pl.when((dist > 0) & (dist < SPAN))
    def _():
        near(1)

    @pl.when(dist == SPAN)
    def _():
        near(2)

    @pl.when((dist < 0) | (dist > SPAN))
    def _():
        acc[...] = jnp.zeros_like(acc)
        lref[...] = jnp.zeros_like(lref)
        mref[...] = jnp.full_like(mref, LOW)

    number = table_ref[src, capacity]

    def slots(i, carry):
        work = []
        for j in range(2):
            at_slot = 2 * i + j
            packed = table_ref[src, at_slot]
            at = pl.ds(pl.multiple_of((packed // blocks_held) * QBLK, QBLK), QBLK)
            mat = pl.ds(pl.multiple_of((packed % blocks_held) * QBLK, QBLK), QBLK)
            for h in range(heads):
                work.append((at, mat, slice(h * size, (h + 1) * size), h, at_slot < number))
        raw = [
            lax.dot_general(q_ref[0, at, cols], mk_ref[mat, cols], NT, preferred_element_type=jnp.float32)
            for at, mat, cols, h, real in work
        ]
        raw = [
            jnp.where(real, s * scale + gate_ref[h] * LOG2E, 2 * LOW)
            for s, (at, mat, cols, h, real) in zip(raw, work)
        ]
        tops = [jnp.max(s, axis=1, keepdims=True) for s in raw]
        probs = [jnp.exp2(s - top).astype(jnp.bfloat16) for s, top in zip(raw, tops)]
        ones = jnp.ones((QBLK, size), jnp.bfloat16)
        sums = [
            jnp.dot(p, jnp.concatenate([mv_ref[mat, cols], ones], axis=1), preferred_element_type=jnp.float32)
            for p, (at, mat, cols, h, real) in zip(probs, work)
        ]
        for top, both, (at, mat, cols, h, real) in zip(tops, sums, work):
            old = mref[at, cols]
            new = jnp.maximum(old, top)
            keep = jnp.exp2(old - new)
            add = jnp.exp2(top - new)
            acc[at, cols] = acc[at, cols] * keep + both[:, :size] * add
            lref[at, cols] = lref[at, cols] * keep + both[:, size:] * add
            mref[at, cols] = new
        return carry

    lax.fori_loop(0, (number + 1) // 2, slots, 0)

    step = 128

    @pl.loop(0, rows // step)
    def _(r):
        at = pl.ds(pl.multiple_of(r * step, step), step)
        lane = lax.broadcasted_iota(jnp.int32, (step, 128), 1)
        tops = jnp.full((step, 128), LOW, jnp.float32)
        sums = jnp.ones((step, 128), jnp.float32)
        for h in range(heads):
            cols = slice(h * size, (h + 1) * size)
            l = lref[at, cols]
            safe = jnp.where(l > 0.0, l, 1.0)
            o_ref[0, at, cols] = (acc[at, cols] / safe).astype(jnp.bfloat16)
            tops = jnp.where(lane == h, mref[at, cols], tops)
            sums = jnp.where(lane == h, safe, sums)
        lse_ref[0, :, at] = (tops + jnp.log2(sums)).T[: lse_ref.shape[1]]


def partials(q_all, keys, values, mkeys, mvalues, gate, place, table, capacity, group):
    sources, _, width = q_all.shape
    rows = keys.shape[0]
    heads = gate.shape[0]
    stat_rows = -(-heads // 8) * 8
    side = lambda a: pl.BlockSpec((a.shape[0], width), lambda s: (0, group))
    smem = pl.BlockSpec(memory_space=pltpu.SMEM)
    per = pl.BlockSpec((1, rows, width), lambda s: (s, 0, 0))
    return pl.pallas_call(
        functools.partial(local_kernel, heads, mkeys.shape[0] // QBLK, capacity),
        grid=(sources,),
        in_specs=[smem, smem, smem, per, side(keys), side(values), side(mkeys), side(mvalues)],
        out_specs=[per, pl.BlockSpec((1, stat_rows, rows), lambda s: (s, 0, 0))],
        out_shape=[
            jax.ShapeDtypeStruct((sources, rows, width), jnp.bfloat16),
            jax.ShapeDtypeStruct((sources, stat_rows, rows), jnp.float32),
        ],
        scratch_shapes=[pltpu.VMEM((rows, width), jnp.float32)] * 3,
        compiler_params=pltpu.CompilerParams(vmem_limit_bytes=56 * 2**20),
        cost_estimate=pl.CostEstimate(
            flops=20 * rows * rows * width, bytes_accessed=64 * rows * width, transcendentals=rows * rows * heads
        ),
    )(place, table, gate, q_all, keys, values, mkeys, mvalues)


def merge_kernel(
    heads, chips, halves, o_a, lse_a, o_b, lse_b, out_ref,
    own, own_s, twin, twin_s, left, left_s, right, right_s,
    load_sem, load_s_sem, tsend, tsend_s, trecv, trecv_s,
    usend, usend_s, urecv, urecv_s, dsend, dsend_s, drecv, drecv_s,
):
    c = lax.axis_index("ctx")
    m = lax.axis_index("mem")
    rows, width = out_ref.shape
    size = width // heads
    half = rows // halves
    wide = width // 2
    last = chips - 1
    hbm = ((o_a, lse_a), (o_b, lse_b))

    barrier = pltpu.get_barrier_semaphore()
    pl.semaphore_signal(barrier, inc=1, device_id={"mem": 1 - m}, device_id_type=MESH)

    @pl.when(c > 0)
    def _():
        pl.semaphore_signal(barrier, inc=1, device_id={"ctx": c - 1}, device_id_type=MESH)

    @pl.when(c < last)
    def _():
        pl.semaphore_signal(barrier, inc=1, device_id={"ctx": c + 1}, device_id_type=MESH)

    inner = (c > 0).astype(jnp.int32) + (c < last).astype(jnp.int32)
    pl.semaphore_wait(barrier, 1 + inner)

    def remote(src, dst, ss, rs, where):
        return pltpu.make_async_remote_copy(
            src_ref=src, dst_ref=dst, send_sem=ss, recv_sem=rs, device_id=where, device_id_type=MESH
        )

    def spots(g, d, r):
        at = pl.ds(pl.multiple_of(r * half, half), half)
        return (g, d, at), (g, d, slice(None), at), (at, (slice(None), at)), (g * chips + d) * halves + r

    def loads(g, d, r):
        big, small, (at, at_s), n = spots(g, d, r)
        o_hbm, lse_hbm = hbm[g]
        return (
            pltpu.make_async_copy(o_hbm.at[2 * d + m, at], own.at[big], load_sem.at[n]),
            pltpu.make_async_copy(lse_hbm.at[2 * d + m, :, at], own_s.at[small], load_s_sem.at[n]),
        )

    def twins(g, d, r):
        big, small, (at, at_s), n = spots(g, d, r)
        o_hbm, lse_hbm = hbm[g]
        other = {"mem": 1 - m}
        return (
            remote(o_hbm.at[2 * d + 1 - m, at], twin.at[big], tsend.at[n], trecv.at[n], other),
            remote(lse_hbm.at[2 * d + 1 - m, :, at], twin_s.at[small], tsend_s.at[n], trecv_s.at[n], other),
        )

    def ups(g, d, r):
        big, small, _, n = spots(g, d, r)
        where = {"ctx": c + 1}
        return (
            remote(own.at[big], left.at[big], usend.at[n], urecv.at[n], where),
            remote(own_s.at[small], left_s.at[small], usend_s.at[n], urecv_s.at[n], where),
        )

    def downs(g, d, r):
        big, small, _, n = spots(g, d, r)
        where = {"ctx": c - 1}
        return (
            remote(own.at[big], right.at[big], dsend.at[n], drecv.at[n], where),
            remote(own_s.at[small], right_s.at[small], dsend_s.at[n], drecv_s.at[n], where),
        )

    order = []
    for i in range(chips):
        for d in (last - i, i):
            if d not in order:
                order.append(d)
    for d in order:
        for g in range(2):
            @pl.loop(0, halves)
            def _(r):
                for copy in twins(g, d, r) + loads(g, d, r):
                    copy.start()

    def combine(g, d, r, into, others):
        big, small, _, _ = spots(g, d, r)
        parts = [own] + [o for o, _ in others]
        stats = [own_s[small]] + [s[small] for _, s in others]
        top = functools.reduce(jnp.maximum, stats)
        weights = [jnp.exp2(s - top) for s in stats]
        total = functools.reduce(jnp.add, weights)
        own_s[small] = top + jnp.log2(total)
        shares = [(w / total).T for w in weights]
        step = 64
        for t in range(half // step):
            at = pl.ds(pl.multiple_of(r * half + t * step, step), step)
            for h in range(heads // 2):
                cols = slice(h * size, (h + 1) * size)
                out = None
                for part, share in zip(parts, shares):
                    term = part[g, d, at, cols].astype(jnp.float32) * share[t * step : (t + 1) * step, h : h + 1]
                    out = term if out is None else out + term
                into(at, cols, out.astype(jnp.bfloat16))

    def wait_local(g, d, r):
        for copy in loads(g, d, r):
            copy.wait()
        for copy in twins(g, d, r):
            copy.wait()

    def store_own(g, d):
        def put(at, cols, value):
            own[g, d, at, cols] = value
        return put

    def store_out(g):
        def put(at, cols, value):
            out_ref[at, g * wide + cols.start : g * wide + cols.stop] = value
        return put

    def visit(g, d, r, copies, first, arrived):
        wait_local(g, d, r)

        @pl.when(first)
        def _():
            combine(g, d, r, store_own(g, d), [(twin, twin_s)])

        @pl.when(jnp.logical_not(first))
        def _():
            for copy in copies(g, d, r):
                copy.wait_recv()
            combine(g, d, r, store_own(g, d), [(twin, twin_s), arrived])

        for copy in copies(g, d, r):
            copy.start()

    @pl.loop(0, last)
    def _(i):
        for g in range(2):
            @pl.loop(0, halves)
            def _(r):
                @pl.when(last - i > c)
                def _():
                    visit(g, last - i, r, ups, c == 0, (left, left_s))

                @pl.when(i < c)
                def _():
                    visit(g, i, r, downs, c == last, (right, right_s))

    for g in range(2):
        @pl.loop(0, halves)
        def _(r):
            wait_local(g, c, r)

            @pl.when(c == 0)
            def _():
                for copy in downs(g, c, r):
                    copy.wait_recv()
                combine(g, c, r, store_out(g), [(twin, twin_s), (right, right_s)])

            @pl.when(c == last)
            def _():
                for copy in ups(g, c, r):
                    copy.wait_recv()
                combine(g, c, r, store_out(g), [(twin, twin_s), (left, left_s)])

            @pl.when((c > 0) & (c < last))
            def _():
                for copy in ups(g, c, r) + downs(g, c, r):
                    copy.wait_recv()
                combine(g, c, r, store_out(g), [(twin, twin_s), (left, left_s), (right, right_s)])

    @pl.loop(0, chips)
    def _(d):
        for g in range(2):
            @pl.loop(0, halves)
            def _(r):
                @pl.when(d > c)
                def _():
                    for copy in ups(g, d, r):
                        copy.wait_send()

                @pl.when(d < c)
                def _():
                    for copy in downs(g, d, r):
                        copy.wait_send()


def merged(first, second, heads):
    (o_a, lse_a), (o_b, lse_b) = first, second
    sources, rows, width = o_a.shape
    chips = sources // 2
    halves = 4 if chips <= 4 else 1
    big = pltpu.VMEM((2, chips, rows, width), jnp.bfloat16)
    small = pltpu.VMEM((2, chips) + lse_a.shape[1:], jnp.float32)
    return pl.pallas_call(
        functools.partial(merge_kernel, heads, chips, halves),
        in_specs=[pl.BlockSpec(memory_space=pl.ANY)] * 4,
        out_specs=pl.BlockSpec(memory_space=pltpu.VMEM),
        out_shape=jax.ShapeDtypeStruct((rows, 2 * width), jnp.bfloat16),
        scratch_shapes=[big, small] * 4 + [pltpu.SemaphoreType.DMA((2 * chips * halves,))] * 14,
        compiler_params=pltpu.CompilerParams(
            collective_id=0, has_side_effects=True, vmem_limit_bytes=56 * 2**20
        ),
    )(o_a, lse_a, o_b, lse_b)


def gather_kernel(chips, q_ref, out_ref, own_sem, usend, urecv, dsend, drecv, tsend, trecv):
    c = lax.axis_index("ctx")
    m = lax.axis_index("mem")
    last = chips - 1
    barrier = pltpu.get_barrier_semaphore()
    pl.semaphore_signal(barrier, inc=1, device_id={"mem": 1 - m}, device_id_type=MESH)

    @pl.when(c > 0)
    def _():
        pl.semaphore_signal(barrier, inc=1, device_id={"ctx": c - 1}, device_id_type=MESH)

    @pl.when(c < last)
    def _():
        pl.semaphore_signal(barrier, inc=1, device_id={"ctx": c + 1}, device_id_type=MESH)

    inner = (c > 0).astype(jnp.int32) + (c < last).astype(jnp.int32)
    pl.semaphore_wait(barrier, 1 + inner)

    def copy(src, d, sends, recvs, where):
        return pltpu.make_async_remote_copy(
            src_ref=src, dst_ref=out_ref.at[2 * d + m], send_sem=sends.at[d], recv_sem=recvs.at[d],
            device_id=where, device_id_type=MESH,
        )

    def up(src, d):
        return copy(src, d, usend, urecv, {"ctx": c + 1})

    def down(src, d):
        return copy(src, d, dsend, drecv, {"ctx": c - 1})

    def twin(src, d):
        return copy(src, d, tsend, trecv, {"mem": 1 - m})

    @pl.when(c < last)
    def _():
        up(q_ref, c).start()

    @pl.when(c > 0)
    def _():
        down(q_ref, c).start()

    twin(q_ref, c).start()
    own = pltpu.make_async_copy(q_ref, out_ref.at[2 * c + m], own_sem)
    own.start()

    @pl.loop(0, last)
    def _(t):
        low = c - 1 - t
        high = c + 1 + t

        @pl.when(low >= 0)
        def _():
            block = out_ref.at[2 * low + m]
            up(block, low).wait_recv()

            @pl.when(c < last)
            def _():
                up(block, low).start()

            twin(block, low).start()

        @pl.when(high <= last)
        def _():
            block = out_ref.at[2 * high + m]
            down(block, high).wait_recv()

            @pl.when(c > 0)
            def _():
                down(block, high).start()

            twin(block, high).start()

    own.wait()

    @pl.loop(0, chips)
    def _(d):
        twin(q_ref, d).wait()

        @pl.when((d <= c) & (c < last))
        def _():
            up(q_ref, d).wait_send()

        @pl.when((d >= c) & (c > 0))
        def _():
            down(q_ref, d).wait_send()


def gathered(q, sources):
    chips = sources // 2
    return pl.pallas_call(
        functools.partial(gather_kernel, chips),
        in_specs=[pl.BlockSpec(memory_space=pl.ANY)],
        out_specs=pl.BlockSpec(memory_space=pl.ANY),
        out_shape=jax.ShapeDtypeStruct((sources,) + q.shape, q.dtype),
        scratch_shapes=[pltpu.SemaphoreType.DMA] + [pltpu.SemaphoreType.DMA((chips,))] * 6,
        compiler_params=pltpu.CompilerParams(collective_id=1, has_side_effects=True),
    )(q)


def body(queries, keys, values, memory_keys, memory_values, retrieval, memory_gate):
    axes = ("ctx", "mem")
    sources = lax.axis_size(axes)
    place = lax.axis_index(axes)
    query_blocks, topk = retrieval.shape
    capacity = max(3, 3 * query_blocks * topk // (2 * sources))
    blocks_held = memory_keys.shape[0] // QBLK
    heads = memory_gate.shape[0]
    wide = queries.shape[1] // 2
    tok_rows = queries.shape[0]
    ids = retrieval.reshape(1, -1)
    halves = jnp.concatenate([ids // 256, ids % 256], axis=0).astype(queries.dtype)
    tail = jnp.pad(halves, ((0, 14), (0, wide - ids.shape[1])))
    q_a = gathered(jnp.concatenate([queries[:, :wide], tail], axis=0), sources)
    later, q_a = lax.optimization_barrier((queries[:, wide:], q_a))
    q_b = lax.all_gather(later, axes, axis=0)
    got = q_a[:, tok_rows : tok_rows + 2, : ids.shape[1]].astype(jnp.int32)
    everyone = (got[:, 0] * 256 + got[:, 1]).reshape(-1, topk)
    table = slot_tables(everyone, place, blocks_held, sources, capacity)
    where = place.reshape(1).astype(jnp.int32)
    sides = (keys, values, memory_keys, memory_values)
    first = partials(q_a, *sides, memory_gate[: heads // 2], where, table, capacity, 0)
    second = partials(q_b, *sides, memory_gate[heads // 2 :], where, table, capacity, 1)
    return merged(first, second, heads)


def solution(mesh):
    rows = P(("groups", "ctx", "mem"), "head")
    return jax.shard_map(
        body,
        mesh=mesh,
        in_specs=(rows, rows, rows, rows, rows, P(("groups", "ctx", "mem"), None), P("head")),
        out_specs=rows,
        check_vma=False,
    )
```

```python
import functools
import math

import jax
import jax.numpy as jnp
from jax import lax
from jax.experimental import pallas as pl
from jax.experimental.pallas import tpu as pltpu
from jax.sharding import PartitionSpec as P

QBLK = 64
SPAN = 4
LOW = -1e30
LOG2E = math.log2(math.e)
MESH = pl.DeviceIdType.MESH
NT = (((1,), (1,)), ((), ()))


def slot_tables(everyone, place, blocks_held, sources, capacity):
    ids = everyone.reshape(sources, -1)
    topk = everyone.shape[1]
    mine = (ids // blocks_held) == place
    rank = jnp.cumsum(mine.astype(jnp.int32), axis=1) - 1
    slots = jnp.arange(capacity, dtype=jnp.int32)
    match = mine[:, :, None] & (rank[:, :, None] == slots[None, None, :])
    entry = jnp.arange(ids.shape[1], dtype=jnp.int32)[None, :, None]
    packed = (entry // topk) * blocks_held + (ids % blocks_held)[:, :, None]
    table = jnp.sum(jnp.where(match, packed, 0), axis=1)
    count = jnp.sum(mine.astype(jnp.int32), axis=1)
    return jnp.concatenate([table, count[:, None]], axis=1)


def local_kernel(
    heads, blocks_held, capacity, place_ref, table_ref, gate_ref,
    q_ref, k_ref, v_ref, mk_ref, mv_ref, o_ref, lse_ref, acc, mref, lref,
):
    src = pl.program_id(0)
    rows = q_ref.shape[1]
    size = q_ref.shape[2] // heads
    scale = LOG2E / math.sqrt(size)
    dist = src - place_ref[0]

    def near(kind):
        tile = rows // 2

        @pl.loop(0, heads, unroll=2)
        def _(h):
            cols = pl.ds(pl.multiple_of(h * size, size), size)
            for part in range(2):
                first, count = 0, rows
                if kind == 0 and part == 0:
                    count = tile
                if kind == 2 and part == 1:
                    first, count = tile, tile
                at = pl.ds(part * tile, tile)
                seen = pl.ds(first, count)
                s = lax.dot_general(q_ref[0, at, cols], k_ref[seen, cols], NT, preferred_element_type=jnp.float32)
                if kind != 1:
                    qi = part * tile + lax.broadcasted_iota(jnp.int32, (tile, count), 0)
                    ki = first + lax.broadcasted_iota(jnp.int32, (tile, count), 1)
                    s = jnp.where(ki <= qi if kind == 0 else ki > qi, s, LOW)
                top = jnp.max(s, axis=1, keepdims=True) * scale
                p = jnp.exp2(s * scale - top)
                if kind == 2:
                    p = jnp.where(ki > qi, p, 0.0)
                v = jnp.concatenate([v_ref[seen, cols], jnp.ones((count, size), jnp.bfloat16)], axis=1)
                both = jnp.dot(p.astype(jnp.bfloat16), v, preferred_element_type=jnp.float32)
                acc[at, cols] = both[:, :size]
                lref[at, cols] = both[:, size:]
                mref[at, cols] = jnp.broadcast_to(jnp.maximum(top, LOW), (tile, size))

    @pl.when(dist == 0)
    def _():
        near(0)

    @pl.when((dist > 0) & (dist < SPAN))
    def _():
        near(1)

    @pl.when(dist == SPAN)
    def _():
        near(2)

    @pl.when((dist < 0) | (dist > SPAN))
    def _():
        acc[...] = jnp.zeros_like(acc)
        lref[...] = jnp.zeros_like(lref)
        mref[...] = jnp.full_like(mref, LOW)

    number = table_ref[src, capacity]

    def slots(i, carry):
        work = []
        for j in range(2):
            at_slot = 2 * i + j
            packed = table_ref[src, at_slot]
            at = pl.ds(pl.multiple_of((packed // blocks_held) * QBLK, QBLK), QBLK)
            mat = pl.ds(pl.multiple_of((packed % blocks_held) * QBLK, QBLK), QBLK)
            for h in range(heads):
                work.append((at, mat, slice(h * size, (h + 1) * size), h, at_slot < number))
        raw = [
            lax.dot_general(q_ref[0, at, cols], mk_ref[mat, cols], NT, preferred_element_type=jnp.float32)
            for at, mat, cols, h, real in work
        ]
        raw = [
            jnp.where(real, s * scale + gate_ref[h] * LOG2E, 2 * LOW)
            for s, (at, mat, cols, h, real) in zip(raw, work)
        ]
        tops = [jnp.max(s, axis=1, keepdims=True) for s in raw]
        probs = [jnp.exp2(s - top).astype(jnp.bfloat16) for s, top in zip(raw, tops)]
        ones = jnp.ones((QBLK, size), jnp.bfloat16)
        sums = [
            jnp.dot(p, jnp.concatenate([mv_ref[mat, cols], ones], axis=1), preferred_element_type=jnp.float32)
            for p, (at, mat, cols, h, real) in zip(probs, work)
        ]
        for top, both, (at, mat, cols, h, real) in zip(tops, sums, work):
            old = mref[at, cols]
            new = jnp.maximum(old, top)
            keep = jnp.exp2(old - new)
            add = jnp.exp2(top - new)
            acc[at, cols] = acc[at, cols] * keep + both[:, :size] * add
            lref[at, cols] = lref[at, cols] * keep + both[:, size:] * add
            mref[at, cols] = new
        return carry

    lax.fori_loop(0, (number + 1) // 2, slots, 0)

    step = 128

    @pl.loop(0, rows // step)
    def _(r):
        at = pl.ds(pl.multiple_of(r * step, step), step)
        lane = lax.broadcasted_iota(jnp.int32, (step, 128), 1)
        tops = jnp.full((step, 128), LOW, jnp.float32)
        sums = jnp.ones((step, 128), jnp.float32)
        for h in range(heads):
            cols = slice(h * size, (h + 1) * size)
            l = lref[at, cols]
            safe = jnp.where(l > 0.0, l, 1.0)
            o_ref[0, at, cols] = (acc[at, cols] / safe).astype(jnp.bfloat16)
            tops = jnp.where(lane == h, mref[at, cols], tops)
            sums = jnp.where(lane == h, safe, sums)
        lse_ref[0, :, at] = (tops + jnp.log2(sums)).T[: lse_ref.shape[1]]


def partials(q_all, keys, values, mkeys, mvalues, gate, place, table, capacity, group):
    sources, _, width = q_all.shape
    rows = keys.shape[0]
    heads = gate.shape[0]
    stat_rows = -(-heads // 8) * 8
    side = lambda a: pl.BlockSpec((a.shape[0], width), lambda s: (0, group))
    smem = pl.BlockSpec(memory_space=pltpu.SMEM)
    per = pl.BlockSpec((1, rows, width), lambda s: (s, 0, 0))
    return pl.pallas_call(
        functools.partial(local_kernel, heads, mkeys.shape[0] // QBLK, capacity),
        grid=(sources,),
        in_specs=[smem, smem, smem, per, side(keys), side(values), side(mkeys), side(mvalues)],
        out_specs=[per, pl.BlockSpec((1, stat_rows, rows), lambda s: (s, 0, 0))],
        out_shape=[
            jax.ShapeDtypeStruct((sources, rows, width), jnp.bfloat16),
            jax.ShapeDtypeStruct((sources, stat_rows, rows), jnp.float32),
        ],
        scratch_shapes=[pltpu.VMEM((rows, width), jnp.float32)] * 3,
        compiler_params=pltpu.CompilerParams(vmem_limit_bytes=56 * 2**20),
        cost_estimate=pl.CostEstimate(
            flops=20 * rows * rows * width, bytes_accessed=64 * rows * width, transcendentals=rows * rows * heads
        ),
    )(place, table, gate, q_all, keys, values, mkeys, mvalues)


def merge_kernel(
    heads, chips, halves, o_a, lse_a, o_b, lse_b, out_ref,
    own, own_s, twin, twin_s, left, left_s, right, right_s,
    load_sem, load_s_sem, tsend, tsend_s, trecv, trecv_s,
    usend, usend_s, urecv, urecv_s, dsend, dsend_s, drecv, drecv_s,
):
    c = lax.axis_index("ctx")
    m = lax.axis_index("mem")
    rows, width = out_ref.shape
    size = width // heads
    half = rows // halves
    wide = width // 2
    last = chips - 1
    hbm = ((o_a, lse_a), (o_b, lse_b))

    barrier = pltpu.get_barrier_semaphore()
    pl.semaphore_signal(barrier, inc=1, device_id={"mem": 1 - m}, device_id_type=MESH)

    @pl.when(c > 0)
    def _():
        pl.semaphore_signal(barrier, inc=1, device_id={"ctx": c - 1}, device_id_type=MESH)

    @pl.when(c < last)
    def _():
        pl.semaphore_signal(barrier, inc=1, device_id={"ctx": c + 1}, device_id_type=MESH)

    inner = (c > 0).astype(jnp.int32) + (c < last).astype(jnp.int32)
    pl.semaphore_wait(barrier, 1 + inner)

    def remote(src, dst, ss, rs, where):
        return pltpu.make_async_remote_copy(
            src_ref=src, dst_ref=dst, send_sem=ss, recv_sem=rs, device_id=where, device_id_type=MESH
        )

    def spots(g, d, r):
        at = pl.ds(pl.multiple_of(r * half, half), half)
        return (g, d, at), (g, d, slice(None), at), (at, (slice(None), at)), (g * chips + d) * halves + r

    def loads(g, d, r):
        big, small, (at, at_s), n = spots(g, d, r)
        o_hbm, lse_hbm = hbm[g]
        return (
            pltpu.make_async_copy(o_hbm.at[2 * d + m, at], own.at[big], load_sem.at[n]),
            pltpu.make_async_copy(lse_hbm.at[2 * d + m, :, at], own_s.at[small], load_s_sem.at[n]),
        )

    def twins(g, d, r):
        big, small, (at, at_s), n = spots(g, d, r)
        o_hbm, lse_hbm = hbm[g]
        other = {"mem": 1 - m}
        return (
            remote(o_hbm.at[2 * d + 1 - m, at], twin.at[big], tsend.at[n], trecv.at[n], other),
            remote(lse_hbm.at[2 * d + 1 - m, :, at], twin_s.at[small], tsend_s.at[n], trecv_s.at[n], other),
        )

    def ups(g, d, r):
        big, small, _, n = spots(g, d, r)
        where = {"ctx": c + 1}
        return (
            remote(own.at[big], left.at[big], usend.at[n], urecv.at[n], where),
            remote(own_s.at[small], left_s.at[small], usend_s.at[n], urecv_s.at[n], where),
        )

    def downs(g, d, r):
        big, small, _, n = spots(g, d, r)
        where = {"ctx": c - 1}
        return (
            remote(own.at[big], right.at[big], dsend.at[n], drecv.at[n], where),
            remote(own_s.at[small], right_s.at[small], dsend_s.at[n], drecv_s.at[n], where),
        )

    order = []
    for i in range(chips):
        for d in (last - i, i):
            if d not in order:
                order.append(d)
    for d in order:
        for g in range(2):
            @pl.loop(0, halves)
            def _(r):
                for copy in twins(g, d, r) + loads(g, d, r):
                    copy.start()

    def combine(g, d, r, into, others):
        big, small, _, _ = spots(g, d, r)
        parts = [own] + [o for o, _ in others]
        stats = [own_s[small]] + [s[small] for _, s in others]
        top = functools.reduce(jnp.maximum, stats)
        weights = [jnp.exp2(s - top) for s in stats]
        total = functools.reduce(jnp.add, weights)
        own_s[small] = top + jnp.log2(total)
        shares = [(w / total).T for w in weights]
        step = 64
        for t in range(half // step):
            at = pl.ds(pl.multiple_of(r * half + t * step, step), step)
            for h in range(heads // 2):
                cols = slice(h * size, (h + 1) * size)
                out = None
                for part, share in zip(parts, shares):
                    term = part[g, d, at, cols].astype(jnp.float32) * share[t * step : (t + 1) * step, h : h + 1]
                    out = term if out is None else out + term
                into(at, cols, out.astype(jnp.bfloat16))

    def wait_local(g, d, r):
        for copy in loads(g, d, r):
            copy.wait()
        for copy in twins(g, d, r):
            copy.wait()

    def store_own(g, d):
        def put(at, cols, value):
            own[g, d, at, cols] = value
        return put

    def store_out(g):
        def put(at, cols, value):
            out_ref[at, g * wide + cols.start : g * wide + cols.stop] = value
        return put

    def visit(g, d, r, copies, first, arrived):
        wait_local(g, d, r)

        @pl.when(first)
        def _():
            combine(g, d, r, store_own(g, d), [(twin, twin_s)])

        @pl.when(jnp.logical_not(first))
        def _():
            for copy in copies(g, d, r):
                copy.wait_recv()
            combine(g, d, r, store_own(g, d), [(twin, twin_s), arrived])

        for copy in copies(g, d, r):
            copy.start()

    @pl.loop(0, last)
    def _(i):
        for g in range(2):
            @pl.loop(0, halves)
            def _(r):
                @pl.when(last - i > c)
                def _():
                    visit(g, last - i, r, ups, c == 0, (left, left_s))

                @pl.when(i < c)
                def _():
                    visit(g, i, r, downs, c == last, (right, right_s))

    for g in range(2):
        @pl.loop(0, halves)
        def _(r):
            wait_local(g, c, r)

            @pl.when(c == 0)
            def _():
                for copy in downs(g, c, r):
                    copy.wait_recv()
                combine(g, c, r, store_out(g), [(twin, twin_s), (right, right_s)])

            @pl.when(c == last)
            def _():
                for copy in ups(g, c, r):
                    copy.wait_recv()
                combine(g, c, r, store_out(g), [(twin, twin_s), (left, left_s)])

            @pl.when((c > 0) & (c < last))
            def _():
                for copy in ups(g, c, r) + downs(g, c, r):
                    copy.wait_recv()
                combine(g, c, r, store_out(g), [(twin, twin_s), (left, left_s), (right, right_s)])

    @pl.loop(0, chips)
    def _(d):
        for g in range(2):
            @pl.loop(0, halves)
            def _(r):
                @pl.when(d > c)
                def _():
                    for copy in ups(g, d, r):
                        copy.wait_send()

                @pl.when(d < c)
                def _():
                    for copy in downs(g, d, r):
                        copy.wait_send()


def merged(first, second, heads):
    (o_a, lse_a), (o_b, lse_b) = first, second
    sources, rows, width = o_a.shape
    chips = sources // 2
    halves = 1
    big = pltpu.VMEM((2, chips, rows, width), jnp.bfloat16)
    small = pltpu.VMEM((2, chips) + lse_a.shape[1:], jnp.float32)
    return pl.pallas_call(
        functools.partial(merge_kernel, heads, chips, halves),
        in_specs=[pl.BlockSpec(memory_space=pl.ANY)] * 4,
        out_specs=pl.BlockSpec(memory_space=pltpu.VMEM),
        out_shape=jax.ShapeDtypeStruct((rows, 2 * width), jnp.bfloat16),
        scratch_shapes=[big, small] * 4 + [pltpu.SemaphoreType.DMA((2 * chips * halves,))] * 14,
        compiler_params=pltpu.CompilerParams(
            collective_id=0, has_side_effects=True, vmem_limit_bytes=56 * 2**20
        ),
    )(o_a, lse_a, o_b, lse_b)


def gather_kernel(chips, q_ref, out_ref, own_sem, usend, urecv, dsend, drecv, tsend, trecv):
    c = lax.axis_index("ctx")
    m = lax.axis_index("mem")
    last = chips - 1
    barrier = pltpu.get_barrier_semaphore()
    pl.semaphore_signal(barrier, inc=1, device_id={"mem": 1 - m}, device_id_type=MESH)

    @pl.when(c > 0)
    def _():
        pl.semaphore_signal(barrier, inc=1, device_id={"ctx": c - 1}, device_id_type=MESH)

    @pl.when(c < last)
    def _():
        pl.semaphore_signal(barrier, inc=1, device_id={"ctx": c + 1}, device_id_type=MESH)

    inner = (c > 0).astype(jnp.int32) + (c < last).astype(jnp.int32)
    pl.semaphore_wait(barrier, 1 + inner)

    def copy(src, d, sends, recvs, where):
        return pltpu.make_async_remote_copy(
            src_ref=src, dst_ref=out_ref.at[2 * d + m], send_sem=sends.at[d], recv_sem=recvs.at[d],
            device_id=where, device_id_type=MESH,
        )

    def up(src, d):
        return copy(src, d, usend, urecv, {"ctx": c + 1})

    def down(src, d):
        return copy(src, d, dsend, drecv, {"ctx": c - 1})

    def twin(src, d):
        return copy(src, d, tsend, trecv, {"mem": 1 - m})

    @pl.when(c < last)
    def _():
        up(q_ref, c).start()

    @pl.when(c > 0)
    def _():
        down(q_ref, c).start()

    twin(q_ref, c).start()
    own = pltpu.make_async_copy(q_ref, out_ref.at[2 * c + m], own_sem)
    own.start()

    @pl.loop(0, last)
    def _(t):
        low = c - 1 - t
        high = c + 1 + t

        @pl.when(low >= 0)
        def _():
            block = out_ref.at[2 * low + m]
            up(block, low).wait_recv()

            @pl.when(c < last)
            def _():
                up(block, low).start()

            twin(block, low).start()

        @pl.when(high <= last)
        def _():
            block = out_ref.at[2 * high + m]
            down(block, high).wait_recv()

            @pl.when(c > 0)
            def _():
                down(block, high).start()

            twin(block, high).start()

    own.wait()

    @pl.loop(0, chips)
    def _(d):
        twin(q_ref, d).wait()

        @pl.when((d <= c) & (c < last))
        def _():
            up(q_ref, d).wait_send()

        @pl.when((d >= c) & (c > 0))
        def _():
            down(q_ref, d).wait_send()


def gathered(q, sources):
    chips = sources // 2
    return pl.pallas_call(
        functools.partial(gather_kernel, chips),
        in_specs=[pl.BlockSpec(memory_space=pl.ANY)],
        out_specs=pl.BlockSpec(memory_space=pl.ANY),
        out_shape=jax.ShapeDtypeStruct((sources,) + q.shape, q.dtype),
        scratch_shapes=[pltpu.SemaphoreType.DMA] + [pltpu.SemaphoreType.DMA((chips,))] * 6,
        compiler_params=pltpu.CompilerParams(collective_id=1, has_side_effects=True),
    )(q)


def body(queries, keys, values, memory_keys, memory_values, retrieval, memory_gate):
    axes = ("ctx", "mem")
    sources = lax.axis_size(axes)
    place = lax.axis_index(axes)
    query_blocks, topk = retrieval.shape
    capacity = max(3, 3 * query_blocks * topk // (2 * sources))
    blocks_held = memory_keys.shape[0] // QBLK
    heads = memory_gate.shape[0]
    wide = queries.shape[1] // 2
    tok_rows = queries.shape[0]
    ids = retrieval.reshape(1, -1)
    halves = jnp.concatenate([ids // 256, ids % 256], axis=0).astype(queries.dtype)
    tail = jnp.pad(halves, ((0, 14), (0, wide - ids.shape[1])))
    q_a = gathered(jnp.concatenate([queries[:, :wide], tail], axis=0), sources)
    later, q_a = lax.optimization_barrier((queries[:, wide:], q_a))
    q_b = lax.all_gather(later, axes, axis=0)
    got = q_a[:, tok_rows : tok_rows + 2, : ids.shape[1]].astype(jnp.int32)
    everyone = (got[:, 0] * 256 + got[:, 1]).reshape(-1, topk)
    table = slot_tables(everyone, place, blocks_held, sources, capacity)
    where = place.reshape(1).astype(jnp.int32)
    sides = (keys, values, memory_keys, memory_values)
    first = partials(q_a, *sides, memory_gate[: heads // 2], where, table, capacity, 0)
    second = partials(q_b, *sides, memory_gate[heads // 2 :], where, table, capacity, 1)
    return merged(first, second, heads)


def solution(mesh):
    rows = P(("groups", "ctx", "mem"), "head")
    return jax.shard_map(
        body,
        mesh=mesh,
        in_specs=(rows, rows, rows, rows, rows, P(("groups", "ctx", "mem"), None), P("head")),
        out_specs=rows,
        check_vma=False,
    )
```
